32 devices in a mesh: groups: 2 (over x), graph: 16 (over z, y, core).
Axes of the slice: x: 2, y: 2, z: 4, core: 2. Of those that a mesh axis runs over, the one named last changes fastest.
Arguments:
- node_feat: bfloat16 [8192, 512], P(('groups', 'graph')), parts along dimension 0, may hold values from -6 to 6
- edge_feat: bfloat16 [12288, 512], P(('groups', 'graph')), parts along dimension 0, may hold values from -6 to 6
- edge_source: int32 [12288], P(('groups', 'graph')), parts along dimension 0, may hold values from 0 to 383
- edge_target: int32 [12288], P(('groups', 'graph')), parts along dimension 0, may hold values from 0 to 255
- halo_rows: int32 [32, 16, 8], P(('groups', 'graph')), parts along dimension 0, may hold values from 0 to 255
- edge_count: int32 [32], P(('groups', 'graph')), parts along dimension 0, may hold values from 1 to 384, 3840 in all
- edge_w1: bfloat16 [1536, 512], replicated, may hold values from -0.15625 to 0.15625
- edge_b1: float32 [512], replicated, may hold values from -3 to 3
- edge_w2: bfloat16 [512, 512], replicated, may hold values from -0.25 to 0.25
- edge_gain: float32 [512], replicated, may hold values from 0.25 to 1.75
- node_w1: bfloat16 [1024, 512], replicated, may hold values from -0.1875 to 0.1875
- node_b1: float32 [512], replicated, may hold values from -3 to 3
- node_w2: bfloat16 [512, 512], replicated, may hold values from -0.25 to 0.25
- node_gain: float32 [512], replicated, may hold values from 0.25 to 1.75
- node_cot: bfloat16 [8192, 512], P(('groups', 'graph')), parts along dimension 0, may hold values from -6 to 6
- edge_cot: bfloat16 [12288, 512], P(('groups', 'graph')), parts along dimension 0, may hold values from -6 to 6
Outputs:
- node_out: bfloat16 [8192, 512], P(('groups', 'graph')), parts along dimension 0
- edge_out: bfloat16 [12288, 512], P(('groups', 'graph')), parts along dimension 0
- node_grad: float32 [8192, 512], P(('groups', 'graph')), parts along dimension 0
- edge_grad: float32 [12288, 512], P(('groups', 'graph')), parts along dimension 0
- grad_edge_w1: float32 [3072, 512], P(('groups', 'graph')), parts along dimension 0
- grad_edge_b1: float32 [1024], P(('groups', 'graph')), parts along dimension 0
- grad_edge_w2: float32 [1024, 512], P(('groups', 'graph')), parts along dimension 0
- grad_edge_gain: float32 [1024], P(('groups', 'graph')), parts along dimension 0
- grad_node_w1: float32 [2048, 512], P(('groups', 'graph')), parts along dimension 0
- grad_node_b1: float32 [1024], P(('groups', 'graph')), parts along dimension 0
- grad_node_w2: float32 [1024, 512], P(('groups', 'graph')), parts along dimension 0
- grad_node_gain: float32 [1024], P(('groups', 'graph')), parts along dimension 0
The draws below stay inside these ranges and needn't reach their ends.
There are 2 independent parts, one for each index of `groups`. The reference program is written for one: setup_inputs(seed, part) draws one part's arguments, and reference() takes and returns one part's arrays. A program takes and returns all parts, laid end to end along the dimension named above; an argument that names none is the same for every part. Nothing has to cross between parts.
Inputs may be any that keep to these rules, and one draw needn't show every extreme that they name: halo_rows[q, p, k] is a row of partition q's own nodes that partition p receives in slot k; rows may repeat. `edge_source`: A value below 256 names an own node of the edge's partition; 256 + q * 8 + k names slot k of the rows received from partition q. `edge_target`: the receiver is an own node of the edge's partition. Partition p's first edge_count[p] edge slots are live, the rest padding; some partition has all 384 live.
All inputs are finite; a program needn't handle non-finite values. No bound on the sum of `edge_count` on one device may be relied on, other than what follows from the above.
Results may differ from the reference program's by a relative error of at most 0.009.
Values may be sent and summed in bfloat16 or wider, within the bound.
A program may use at most 128 MiB of HBM per device.

```python
import math
import jax
import jax.numpy as jnp
import numpy as np
from jax import lax

D = 512
NODES_DEV = 256
EDGES_DEV = 384
SLOT = 8
NODES = 4096
EDGES = 6144
TABLE = 384
N_GRAPH = 16


def place_ends(array, stream_key, least, high):
    index_at = [jax.random.randint(jax.random.fold_in(stream_key, axis), (), 0, length) for axis, length in enumerate(array.shape)]
    longest = array.shape.index(max(array.shape))
    next_to = index_at[:longest] + [(index_at[longest] + 1) % array.shape[longest]] + index_at[longest + 1:]
    return array.at[tuple(index_at)].set(least).at[tuple(next_to)].set(high)


def levels(key, shape, cuts, least, high):
    level = 1.0
    for dim, parts in cuts:
        steps = jax.random.uniform(jax.random.fold_in(jax.random.fold_in(key, 6), dim), (parts,), jnp.float32, least / len(cuts), high / len(cuts))
        level = level * jnp.repeat(jnp.exp(steps), shape[dim] // parts).reshape((-1,) + (1,) * (len(shape) - 1 - dim))
    return level


def split_up(number_of, total, most, slope):
    portions = [(1 << 20) // math.isqrt(rank ** slope) + 1 for rank in range(2, number_of + 1)]
    rest, holding = total - most - (number_of - 1), [1] * (number_of - 1)
    while rest > 0:
        candidates = [i for i in range(number_of - 1) if holding[i] < most]
        pool, budget = sum([portions[i] for i in candidates]), rest
        for i in candidates:
            extra = min(most - holding[i], max(1, budget * portions[i] // pool), rest)
            holding[i] = holding[i] + extra
            rest = rest - extra
    return np.array([most] + holding)


def uneven_parts(stream_key, number_of, total, reach, skew):
    if number_of == 2:
        one = jax.random.randint(stream_key, (), max(1, total - reach), min(reach, total - 1) + 1)
        return jnp.stack([one, total - one])
    lengths = jnp.asarray(split_up(number_of, total, reach, skew), jnp.int32)
    pairs = (number_of - 1) // 2
    donor, receiver = lengths[1:1 + 2 * pairs:2], lengths[2:2 + 2 * pairs:2]
    margin = jnp.minimum(donor - 1, reach - receiver)
    moved = jax.random.randint(jax.random.fold_in(stream_key, 1), (pairs,), 0, 1 << 20) % (margin + 1)
    lengths = lengths.at[1:1 + 2 * pairs:2].set(donor - moved).at[2:2 + 2 * pairs:2].set(receiver + moved)
    return lengths[jax.random.permutation(jax.random.fold_in(stream_key, 2), number_of)]


def gaussian(stream_key, shape, deviation, bound, shards=(), held_as=jnp.bfloat16):
    array = deviation * jax.random.normal(stream_key, shape, jnp.float32)
    if shards:
        array = array * levels(stream_key, shape, shards, -0.22, 0.18)
    return jnp.clip(array, -bound, bound).astype(held_as)


def setup_inputs(seed: int = 0, part: int = 0) -> dict:
    seeds = jax.random.split(jax.random.key(seed), 17)
    part_splits = jax.random.split(jax.random.fold_in(seeds[16], part), 17)
    node_feat = gaussian(part_splits[0], (NODES, D), 1.0, 6.0, ((0, 16),))
    edge_feat = gaussian(part_splits[1], (EDGES, D), 1.0, 6.0, ((0, 16),))
    edge_source = place_ends(jax.random.randint(part_splits[2], (EDGES,), 0, TABLE), jax.random.fold_in(part_splits[2], 1), 0, TABLE - 1).astype(jnp.int32)
    edge_target = place_ends(jax.random.randint(part_splits[3], (EDGES,), 0, NODES_DEV), jax.random.fold_in(part_splits[3], 1), 0, NODES_DEV - 1).astype(jnp.int32)
    halo_rows = place_ends(jax.random.randint(part_splits[4], (N_GRAPH, N_GRAPH, SLOT), 0, NODES_DEV), jax.random.fold_in(part_splits[4], 1), 0, NODES_DEV - 1).astype(jnp.int32)
    edge_count = uneven_parts(part_splits[5], N_GRAPH, N_GRAPH * EDGES_DEV * 5 // 8, EDGES_DEV, 1).astype(jnp.int32)
    edge_w1 = gaussian(seeds[6], (3 * D, D), (3 * D) ** -0.5, 0.15625)
    edge_b1 = gaussian(seeds[7], (D,), 0.5, 3.0, (), jnp.float32)
    edge_w2 = gaussian(seeds[8], (D, D), D ** -0.5, 0.25)
    edge_gain = jnp.clip(1.0 + 0.15 * jax.random.normal(seeds[9], (D,), jnp.float32), 0.25, 1.75)
    node_w1 = gaussian(seeds[10], (2 * D, D), (2 * D) ** -0.5, 0.1875)
    node_b1 = gaussian(seeds[11], (D,), 0.5, 3.0, (), jnp.float32)
    node_w2 = gaussian(seeds[12], (D, D), D ** -0.5, 0.25)
    node_gain = jnp.clip(1.0 + 0.15 * jax.random.normal(seeds[13], (D,), jnp.float32), 0.25, 1.75)
    node_cot = gaussian(part_splits[14], (NODES, D), 1.0, 6.0, ((0, 16),))
    edge_cot = gaussian(part_splits[15], (EDGES, D), 1.0, 6.0, ((0, 16),))
    return {"node_feat": node_feat, "edge_feat": edge_feat, "edge_source": edge_source, "edge_target": edge_target, "halo_rows": halo_rows, "edge_count": edge_count, "edge_w1": edge_w1, "edge_b1": edge_b1, "edge_w2": edge_w2, "edge_gain": edge_gain, "node_w1": node_w1, "node_b1": node_b1, "node_w2": node_w2, "node_gain": node_gain, "node_cot": node_cot, "edge_cot": edge_cot}


def silu_grad(pre):
    sig = jax.nn.sigmoid(pre)
    return sig * (1.0 + pre * (1.0 - sig))

def layer_norm(values):
    centred = values - lax.optimization_barrier(jnp.mean(values, axis=-1, keepdims=True))
    rstd = lax.rsqrt(lax.optimization_barrier(jnp.mean(centred * centred, axis=-1, keepdims=True)) + 1e-05)
    return (centred * rstd, rstd)

def mlp_forward(inputs, first, bias, second):
    pre = jnp.dot(inputs, first, preferred_element_type=jnp.float32) + bias
    active = jax.nn.silu(pre).astype(jnp.bfloat16)
    outer = jnp.dot(active, second, preferred_element_type=jnp.float32)
    normed, rstd = layer_norm(outer)
    return (pre, active, normed, rstd)

def mlp_backward(grad_branch, first, second, gain, pre, normed, rstd):
    grad_gain = lax.optimization_barrier(jnp.sum(grad_branch * normed, axis=0))
    scaled = grad_branch * gain
    grad_outer = (scaled - lax.optimization_barrier(jnp.mean(scaled, axis=-1, keepdims=True)) - normed * lax.optimization_barrier(jnp.mean(scaled * normed, axis=-1, keepdims=True))) * rstd
    grad_outer = grad_outer.astype(jnp.bfloat16)
    grad_active = lax.dot_general(grad_outer, second, (((1,), (1,)), ((), ())), preferred_element_type=jnp.float32)
    grad_pre = (grad_active * silu_grad(pre)).astype(jnp.bfloat16)
    grad_bias = lax.optimization_barrier(jnp.sum(grad_pre.astype(jnp.float32), axis=0))
    grad_inputs = lax.dot_general(grad_pre, first, (((1,), (1,)), ((), ())), preferred_element_type=jnp.float32)
    return (grad_inputs, grad_bias, grad_gain, grad_outer, grad_pre)

def transposed(left, right):
    return lax.dot_general(left, right, (((0,), (0,)), ((), ())), preferred_element_type=jnp.float32)

def reference(node_feat, edge_feat, edge_source, edge_target, halo_rows, edge_count, edge_w1, edge_b1, edge_w2, edge_gain, node_w1, node_b1, node_w2, node_gain, node_cot, edge_cot):
    width = node_feat.shape[1]
    position = jnp.arange(EDGES, dtype=jnp.int32)
    owner = position // EDGES_DEV
    live = (position % EDGES_DEV < edge_count[owner]).astype(jnp.float32)[:, None]
    offset = jnp.maximum(edge_source - NODES_DEV, 0)
    peer = offset // SLOT
    within = offset % SLOT
    halo_local = halo_rows[peer, owner, within]
    senders = jnp.where(edge_source < NODES_DEV, owner * NODES_DEV + edge_source, peer * NODES_DEV + halo_local).astype(jnp.int32)
    receivers = (owner * NODES_DEV + edge_target).astype(jnp.int32)
    edge_inputs = jnp.concatenate([edge_feat, node_feat[senders], node_feat[receivers]], axis=1)
    pre_e, act_e, normed_e, rstd_e = mlp_forward(edge_inputs, edge_w1, edge_b1, edge_w2)
    message = (live * normed_e * edge_gain).astype(jnp.bfloat16)
    edge_out = (edge_feat.astype(jnp.float32) + message.astype(jnp.float32)).astype(jnp.bfloat16)
    agg = jax.ops.segment_sum(message.astype(jnp.float32), receivers, NODES).astype(jnp.bfloat16)
    node_inputs = jnp.concatenate([node_feat, agg], axis=1)
    pre_n, act_n, normed_n, rstd_n = mlp_forward(node_inputs, node_w1, node_b1, node_w2)
    node_out = (node_feat.astype(jnp.float32) + normed_n * node_gain).astype(jnp.bfloat16)
    gin_n, gb_n, gg_n, gout_n, gpre_n = mlp_backward(node_cot.astype(jnp.float32), node_w1, node_w2, node_gain, pre_n, normed_n, rstd_n)
    grad_agg = gin_n[:, width:].astype(jnp.bfloat16)
    grad_message = edge_cot.astype(jnp.float32) + grad_agg[receivers].astype(jnp.float32)
    gin_e, gb_e, gg_e, gout_e, gpre_e = mlp_backward(grad_message * live, edge_w1, edge_w2, edge_gain, pre_e, normed_e, rstd_e)
    edge_grad = edge_cot.astype(jnp.float32) + gin_e[:, :width]
    grad_send = gin_e[:, width:2 * width].astype(jnp.bfloat16).astype(jnp.float32)
    grad_recv = gin_e[:, 2 * width:].astype(jnp.bfloat16).astype(jnp.float32)
    node_grad = node_cot.astype(jnp.float32) + gin_n[:, :width] + jax.ops.segment_sum(grad_send, senders, NODES) + jax.ops.segment_sum(grad_recv, receivers, NODES)
    scale = 1.0 / math.sqrt(EDGES)
    return (node_out, edge_out, node_grad, edge_grad, transposed(edge_inputs, gpre_e) * scale, gb_e * scale, transposed(act_e, gout_e) * scale, gg_e * scale, transposed(node_inputs, gpre_n) * scale, gb_n * scale, transposed(act_n, gout_n) * scale, gg_n * scale)
```

```python
import math

import jax
import jax.numpy as jnp
from jax import lax
from jax.experimental import pallas as pl
from jax.experimental.pallas import tpu as pltpu
from jax.sharding import PartitionSpec as P


def silu_grad(pre):
    sig = jax.nn.sigmoid(pre)
    return sig * (1.0 + pre * (1.0 - sig))


def layer_norm(values):
    centred = values - jnp.mean(values, axis=-1, keepdims=True)
    rstd = lax.rsqrt(jnp.mean(centred * centred, axis=-1, keepdims=True) + 1e-05)
    return (centred * rstd, rstd)


def mlp_forward(inputs, first, bias, second):
    pre = jnp.dot(inputs, first, preferred_element_type=jnp.float32) + bias
    active = jax.nn.silu(pre).astype(jnp.bfloat16)
    outer = jnp.dot(active, second, preferred_element_type=jnp.float32)
    normed, rstd = layer_norm(outer)
    return (pre, active, normed, rstd)


def mlp_backward(grad_branch, first, second, gain, pre, normed, rstd):
    grad_gain = jnp.sum(grad_branch * normed, axis=0)
    scaled = grad_branch * gain
    grad_outer = (
        scaled
        - jnp.mean(scaled, axis=-1, keepdims=True)
        - normed * jnp.mean(scaled * normed, axis=-1, keepdims=True)
    ) * rstd
    grad_outer = grad_outer.astype(jnp.bfloat16)
    grad_active = lax.dot_general(
        grad_outer, second, (((1,), (1,)), ((), ())), preferred_element_type=jnp.float32
    )
    grad_pre = (grad_active * silu_grad(pre)).astype(jnp.bfloat16)
    grad_bias = jnp.sum(grad_pre.astype(jnp.float32), axis=0)
    grad_inputs = lax.dot_general(
        grad_pre, first, (((1,), (1,)), ((), ())), preferred_element_type=jnp.float32
    )
    return (grad_inputs, grad_bias, grad_gain, grad_outer, grad_pre)


def transposed(left, right):
    return lax.dot_general(
        left, right, (((0,), (0,)), ((), ())), preferred_element_type=jnp.float32
    )


def indicator(index, count):
    return (index[:, None] == jnp.arange(count, dtype=jnp.int32)[None, :]).astype(jnp.bfloat16)


def general_on_device(
    node_feat,
    edge_feat,
    edge_source,
    edge_target,
    halo_rows,
    edge_count,
    edge_w1,
    edge_b1,
    edge_w2,
    edge_gain,
    node_w1,
    node_b1,
    node_w2,
    node_gain,
    node_cot,
    edge_cot,
):
    peers = lax.axis_size("graph")
    nodes_local, width = node_feat.shape
    edges_local = edge_feat.shape[0]
    slots = halo_rows.shape[2]
    table_rows = nodes_local + peers * slots
    requests = halo_rows.reshape(-1)
    outgoing = jnp.take(node_feat, requests, axis=0).reshape(peers, slots, width)
    received = lax.all_to_all(outgoing, "graph", split_axis=0, concat_axis=0, tiled=True)
    table = jnp.concatenate([node_feat, received.reshape(peers * slots, width)], axis=0)
    source_hot = indicator(edge_source, table_rows)
    target_hot = indicator(edge_target, nodes_local)
    senders = jnp.dot(source_hot, table, preferred_element_type=jnp.float32).astype(jnp.bfloat16)
    receivers = jnp.dot(target_hot, node_feat, preferred_element_type=jnp.float32).astype(
        jnp.bfloat16
    )
    live = (jnp.arange(edges_local, dtype=jnp.int32) < edge_count[0]).astype(jnp.float32)[:, None]
    edge_inputs = jnp.concatenate([edge_feat, senders, receivers], axis=1)
    pre_e, act_e, normed_e, rstd_e = mlp_forward(edge_inputs, edge_w1, edge_b1, edge_w2)
    message = (live * normed_e * edge_gain).astype(jnp.bfloat16)
    edge_out = (edge_feat.astype(jnp.float32) + message.astype(jnp.float32)).astype(jnp.bfloat16)
    agg = transposed(target_hot, message).astype(jnp.bfloat16)
    node_inputs = jnp.concatenate([node_feat, agg], axis=1)
    pre_n, act_n, normed_n, rstd_n = mlp_forward(node_inputs, node_w1, node_b1, node_w2)
    node_out = (node_feat.astype(jnp.float32) + normed_n * node_gain).astype(jnp.bfloat16)
    gin_n, gb_n, gg_n, gout_n, gpre_n = mlp_backward(
        node_cot.astype(jnp.float32), node_w1, node_w2, node_gain, pre_n, normed_n, rstd_n
    )
    grad_agg = gin_n[:, width:].astype(jnp.bfloat16)
    picked = jnp.dot(target_hot, grad_agg, preferred_element_type=jnp.float32)
    grad_message = edge_cot.astype(jnp.float32) + picked
    gin_e, gb_e, gg_e, gout_e, gpre_e = mlp_backward(
        grad_message * live, edge_w1, edge_w2, edge_gain, pre_e, normed_e, rstd_e
    )
    edge_grad = edge_cot.astype(jnp.float32) + gin_e[:, :width]
    grad_send = gin_e[:, width : 2 * width].astype(jnp.bfloat16)
    grad_recv = gin_e[:, 2 * width :].astype(jnp.bfloat16)
    table_grad = transposed(source_hot, grad_send)
    recv_grad = transposed(target_hot, grad_recv)
    halo_part = table_grad[nodes_local:].reshape(peers, slots, width)
    returned = lax.all_to_all(
        halo_part.astype(jnp.bfloat16), "graph", split_axis=0, concat_axis=0, tiled=True
    ).astype(halo_part.dtype)
    halo_grad = jax.ops.segment_sum(returned.reshape(peers * slots, width), requests, nodes_local)
    node_grad = (
        node_cot.astype(jnp.float32)
        + gin_n[:, :width]
        + table_grad[:nodes_local]
        + recv_grad
        + halo_grad
    )
    scale = 1.0 / math.sqrt(edges_local * peers)
    g_ew1, g_eb1, g_ew2, g_egain, g_nw1, g_nb1, g_nw2, g_ngain = (
        lax.psum_scatter(
            transposed(edge_inputs, gpre_e) * scale, "graph", scatter_dimension=0, tiled=True
        ),
        lax.psum_scatter(gb_e * scale, "graph", scatter_dimension=0, tiled=True),
        lax.psum_scatter(
            transposed(act_e, gout_e) * scale, "graph", scatter_dimension=0, tiled=True
        ),
        lax.psum_scatter(gg_e * scale, "graph", scatter_dimension=0, tiled=True),
        lax.psum_scatter(
            transposed(node_inputs, gpre_n) * scale, "graph", scatter_dimension=0, tiled=True
        ),
        lax.psum_scatter(gb_n * scale, "graph", scatter_dimension=0, tiled=True),
        lax.psum_scatter(
            transposed(act_n, gout_n) * scale, "graph", scatter_dimension=0, tiled=True
        ),
        lax.psum_scatter(gg_n * scale, "graph", scatter_dimension=0, tiled=True),
    )
    return (
        node_out,
        edge_out,
        node_grad,
        edge_grad,
        g_ew1,
        g_eb1,
        g_ew2,
        g_egain,
        g_nw1,
        g_nb1,
        g_nw2,
        g_ngain,
    )


MESH = pl.DeviceIdType.MESH
F32 = jnp.float32
BF16 = jnp.bfloat16


def mm(left, right):
    return jnp.dot(left, right, preferred_element_type=F32)


def mm_nt(left, right):
    return lax.dot_general(left, right, (((1,), (1,)), ((), ())), preferred_element_type=F32)


def remote(src, dst, send_sem, recv_sem, peer):
    return pltpu.make_async_remote_copy(
        src_ref=src,
        dst_ref=dst,
        send_sem=send_sem,
        recv_sem=recv_sem,
        device_id={"graph": peer},
        device_id_type=MESH,
    )


class Scatter:
    def __init__(self, place, refs):
        self.outer, self.inner, self.o, self.i, self.c = place
        self.part, self.rc, self.s1, self.ry, self.s2, self.rz, self.send, self.recv = refs
        self.copies = []

    def index(self, o, i, c):
        return (o * self.inner + i) * 2 + c

    def start(self, value):
        rows, cols = self.part.shape[-2:]
        self.part[...] = value.astype(BF16).reshape(self.outer, self.inner, 2, rows, cols)
        peer = self.index(self.o, self.i, 1 - self.c)
        self.core = remote(
            self.part.at[:, :, 1 - self.c], self.rc, self.send.at[0], self.recv.at[0], peer
        )
        self.core.start()
        self.copies.append(self.core)

    def along_inner(self):
        self.core.wait_recv()
        for o in range(self.outer):
            mine = self.part[o, :, pl.ds(self.c, 1)][:, 0]
            self.s1[o] = (mine.astype(F32) + self.rc[o].astype(F32)).astype(BF16)
        self.inner_copies = []
        for k in range(1, self.inner):
            i = lax.rem(self.i + k, self.inner)
            copy = remote(
                self.s1.at[:, i],
                self.ry.at[k - 1],
                self.send.at[k],
                self.recv.at[k],
                self.index(self.o, i, self.c),
            )
            copy.start()
            self.inner_copies.append(copy)
        self.copies += self.inner_copies

    def along_outer(self):
        for copy in self.inner_copies:
            copy.wait_recv()
        for o in range(self.outer):
            total = self.s1[o, pl.ds(self.i, 1)][0].astype(F32)
            for k in range(self.inner - 1):
                total = total + self.ry[k, o].astype(F32)
            self.s2[o] = total.astype(BF16)
        self.outer_copies = []
        for k in range(1, self.outer):
            o = lax.rem(self.o + k, self.outer)
            slot = self.inner - 1 + k
            copy = remote(
                self.s2.at[o],
                self.rz.at[k - 1],
                self.send.at[slot],
                self.recv.at[slot],
                self.index(o, self.i, self.c),
            )
            copy.start()
            self.outer_copies.append(copy)
        self.copies += self.outer_copies

    def finish(self):
        for copy in self.outer_copies:
            copy.wait_recv()
        total = self.s2[pl.ds(self.o, 1)][0].astype(F32)
        for k in range(self.outer - 1):
            total = total + self.rz[k].astype(F32)
        return total


def norm_backward(scaled, normed, rstd):
    return (
        scaled
        - jnp.mean(scaled, axis=-1, keepdims=True)
        - normed * jnp.mean(scaled * normed, axis=-1, keepdims=True)
    ) * rstd


def one_hot_rows(row, count):
    ids = lax.broadcasted_iota(jnp.int32, (count, row.shape[1]), 0)
    return jnp.where(ids == row, 1.0, 0.0).astype(BF16)


def one_hot_columns(row, count):
    length = row.shape[1]
    column = jnp.broadcast_to(row.astype(F32), (128, length)).T.astype(jnp.int32)
    lanes = lax.broadcasted_iota(jnp.int32, (length, 128), 1)
    parts = [
        jnp.where(column == lanes + start, 1.0, 0.0).astype(BF16) for start in range(0, count, 128)
    ]
    return jnp.concatenate(parts, axis=1)


def halves_to_blocks(rows, peers):
    half = rows.shape[1] // 2
    left = rows[:, :half].reshape(peers, 8, half)
    right = rows[:, half:].reshape(peers, 8, half)
    return jnp.concatenate([left, right], axis=1).astype(BF16)


def blocks_to_halves(blocks):
    peers, _, half = blocks.shape
    wide = blocks.astype(F32)
    left = wide[:, :8].reshape(peers * 8, half)
    right = wide[:, 8:].reshape(peers * 8, half)
    return jnp.concatenate([left, right], axis=1).astype(BF16)


def layer_kernel(peers, outer, inner, n_chunks, *refs):
    (nf, ef, src, tgt, req, cnt, ew1, eb1, ew2, egain, nw1, nb1, nw2, ngain, ncot, ecot) = refs[:16]
    (node_out, edge_out, node_grad, edge_grad, g_ew1, g_ew2, g_nw1, g_nw2, g_small) = refs[16:25]
    (hout, hin, bout, bin_, x_e, pre_e, z_e, rstd_e, act_e, x_n, pre_n, z_n, gpre_n, gpre_e,
     h_send, h_recv, b_send, b_recv) = refs[25:43]
    chunk_refs = refs[43:]
    nodes, width = nf.shape
    edges = ef.shape[0]
    me = lax.axis_index("graph")
    c = lax.rem(me, 2)
    i = lax.rem(me // 2, inner)
    o = me // (2 * inner)
    place = (outer, inner, o, i, c)
    s_nw2, s_nw1, s_ew2, s_e0, s_e1 = [
        Scatter(place, chunk_refs[8 * k : 8 * k + 8]) for k in range(n_chunks)
    ]

    barrier = pltpu.get_barrier_semaphore()
    others = [lax.rem(me + k, peers) for k in range(1, peers)]
    for peer in others:
        pl.semaphore_signal(barrier, inc=1, device_id={"graph": peer}, device_id_type=MESH)

    hout[...] = halves_to_blocks(mm(one_hot_columns(req[...], nodes), nf[...]), peers)
    hin[pl.ds(me, 1)] = hout[pl.ds(me, 1)]
    pl.semaphore_wait(barrier, peers - 1)
    halo = []
    for k, peer in enumerate(others):
        copy = remote(hout.at[peer], hin.at[me], h_send.at[k], h_recv.at[k], peer)
        copy.start()
        halo.append(copy)

    table_rows = nodes + peers * 8
    source_hot = one_hot_columns(src[...], table_rows)
    target_hot = one_hot_columns(tgt[...], nodes)
    target_hot_t = one_hot_rows(tgt[...], nodes)
    live = jnp.where(lax.broadcasted_iota(jnp.int32, (edges, 1), 0) < cnt[0], 1.0, 0.0).astype(F32)
    x_e[:, :width] = ef[...]
    x_e[:, 2 * width :] = mm(target_hot, nf[...]).astype(BF16)
    own = mm(source_hot[:, :nodes], nf[...])
    pre_e[...] = (
        mm(ef[...], ew1[:width]) + mm(x_e[:, 2 * width :], ew1[2 * width :]) + eb1[...]
    )
    x_n[:, :width] = nf[...]
    pre_n[...] = mm(nf[...], nw1[:width]) + nb1[...]

    for copy in halo:
        copy.wait_recv()
    received = blocks_to_halves(hin[...])
    x_e[:, width : 2 * width] = (own + mm(source_hot[:, nodes:], received)).astype(BF16)
    pre = pre_e[...] + mm(x_e[:, width : 2 * width], ew1[width : 2 * width])
    sig = jax.nn.sigmoid(pre)
    act_e[...] = (pre * sig).astype(BF16)
    pre_e[...] = sig * (1.0 + pre * (1.0 - sig))
    normed, rstd = layer_norm(mm(act_e[...], ew2[...]))
    z_e[...] = normed
    rstd_e[...] = rstd
    message = (live * normed * egain[...]).astype(BF16)
    edge_out[...] = (ef[...].astype(F32) + message.astype(F32)).astype(BF16)
    x_n[:, width:] = mm(target_hot_t, message).astype(BF16)

    pre = pre_n[...] + mm(x_n[:, width:], nw1[width:])
    sig = jax.nn.sigmoid(pre)
    act_n = (pre * sig).astype(BF16)
    slope = sig * (1.0 + pre * (1.0 - sig))
    normed, rstd = layer_norm(mm(act_n, nw2[...]))
    node_out[...] = (nf[...].astype(F32) + normed * ngain[...]).astype(BF16)
    grad = ncot[...].astype(F32)
    gg_n = jnp.sum(grad * normed, axis=0, keepdims=True)
    gout = norm_backward(grad * ngain[...], normed, rstd).astype(BF16)
    gpre_n[...] = (mm_nt(gout, nw2[...]) * slope).astype(BF16)
    gb_n = jnp.sum(gpre_n[...].astype(F32), axis=0, keepdims=True)
    grad_agg = mm_nt(gpre_n[...], nw1[width:]).astype(BF16)
    s_nw1.start(transposed(x_n[...], gpre_n[...]))
    s_nw2.start(transposed(act_n, gout))

    grad = live * (ecot[...].astype(F32) + mm(target_hot, grad_agg))
    normed = z_e[...]
    gg_e = jnp.sum(grad * normed, axis=0, keepdims=True)
    gout = norm_backward(grad * egain[...], normed, rstd_e[...]).astype(BF16)
    s_nw1.along_inner()
    s_ew2.start(transposed(act_e[...], gout))
    s_nw2.along_inner()
    gpre_e[...] = (mm_nt(gout, ew2[...]) * pre_e[...]).astype(BF16)
    gb_e = jnp.sum(gpre_e[...].astype(F32), axis=0, keepdims=True)
    half = width // 2
    s_e0.start(transposed(x_e[...], gpre_e[:, :half]))
    s_ew2.along_inner()
    s_nw1.along_outer()
    s_e1.start(transposed(x_e[...], gpre_e[:, half:]))
    s_nw2.along_outer()

    grad_send = mm_nt(gpre_e[...], ew1[width : 2 * width]).astype(BF16)
    source_hot_t = one_hot_rows(src[...], table_rows)
    bout[:, :, :half] = halves_to_blocks(mm(source_hot_t[nodes:], grad_send), peers)
    per = width // peers
    column = lax.broadcasted_iota(jnp.int32, (peers, width), 1)
    owner = lax.broadcasted_iota(jnp.int32, (peers, width), 0) * per
    owned = jnp.logical_and(column >= owner, column < owner + per)
    where_from = lax.rem(lax.broadcasted_iota(jnp.int32, (width, 128), 0), per)
    where_to = lax.broadcasted_iota(jnp.int32, (width, 128), 1)
    small = jnp.zeros((peers, 128), F32)
    for q, vector in enumerate((gb_e, gg_e, gb_n, gg_n)):
        spread = jnp.where(owned, vector, 0.0).astype(BF16)
        move = jnp.where(where_to == where_from + q * per, 1.0, 0.0).astype(BF16)
        small = small + mm(spread, move)
    bout[:, :, half:] = jnp.broadcast_to(small[:, None, :], (peers, 16, 128)).astype(BF16)
    bin_[pl.ds(me, 1)] = bout[pl.ds(me, 1)]
    s_e0.along_inner()
    back = []
    for k, peer in enumerate(others):
        copy = remote(bout.at[peer], bin_.at[me], b_send.at[k], b_recv.at[k], peer)
        copy.start()
        back.append(copy)
    s_e1.along_inner()
    s_ew2.along_outer()

    edge_grad[...] = ecot[...].astype(F32) + mm_nt(gpre_e[...], ew1[:width])
    grad_recv = mm_nt(gpre_e[...], ew1[2 * width :]).astype(BF16)
    s_e0.along_outer()
    node_grad[...] = (
        ncot[...].astype(F32)
        + mm_nt(gpre_n[...], nw1[:width])
        + mm(source_hot_t[:nodes], grad_send)
        + mm(target_hot_t, grad_recv)
    )
    s_e1.along_outer()
    scale = 1.0 / math.sqrt(edges * peers)
    g_nw1[...] = s_nw1.finish() * scale
    g_nw2[...] = s_nw2.finish() * scale
    for copy in back:
        copy.wait_recv()
    node_grad[...] += mm(one_hot_rows(req[...], nodes), blocks_to_halves(bin_[:, :, :half]))
    g_small[...] = jnp.sum(bin_[:, :, half:].astype(F32), axis=0)[:8] * scale
    g_ew2[...] = s_ew2.finish() * scale
    g_ew1[:, :half] = s_e0.finish() * scale
    g_ew1[:, half:] = s_e1.finish() * scale
    for copy in halo + back:
        copy.wait_send()
    for chunk in (s_nw1, s_nw2, s_ew2, s_e0, s_e1):
        for copy in chunk.copies:
            copy.wait_send()


def kernel_fits(peers, width, slots):
    return (
        slots == 8
        and width % (peers * 16) == 0
        and 4 * (width // peers) <= 128
        and peers * slots % 128 == 0
    )


def on_device(
    node_feat,
    edge_feat,
    edge_source,
    edge_target,
    halo_rows,
    edge_count,
    edge_w1,
    edge_b1,
    edge_w2,
    edge_gain,
    node_w1,
    node_b1,
    node_w2,
    node_gain,
    node_cot,
    edge_cot,
):
    peers = lax.axis_size("graph")
    nodes, width = node_feat.shape
    edges = edge_feat.shape[0]
    if not kernel_fits(peers, width, halo_rows.shape[2]):
        return general_on_device(
            node_feat, edge_feat, edge_source, edge_target, halo_rows, edge_count,
            edge_w1, edge_b1, edge_w2, edge_gain, node_w1, node_b1, node_w2, node_gain,
            node_cot, edge_cot,
        )
    inner = 1 << (int(math.log2(peers // 2)) // 2)
    outer = peers // 2 // inner
    shares = [
        (width // peers, width),
        (2 * width // peers, width),
        (width // peers, width),
        (3 * width // peers, width // 2),
        (3 * width // peers, width // 2),
    ]
    chunk_scratch = []
    for rows, cols in shares:
        chunk_scratch += [
            pltpu.VMEM((outer, inner, 2, rows, cols), BF16),
            pltpu.VMEM((outer, inner, rows, cols), BF16),
            pltpu.VMEM((outer, inner, rows, cols), BF16),
            pltpu.VMEM((inner - 1, outer, rows, cols), BF16),
            pltpu.VMEM((outer, rows, cols), BF16),
            pltpu.VMEM((outer - 1, rows, cols), BF16),
            pltpu.SemaphoreType.DMA((inner + outer - 1,)),
            pltpu.SemaphoreType.DMA((inner + outer - 1,)),
        ]
    half = width // 2
    vmem = pl.BlockSpec(memory_space=pltpu.VMEM)
    smem = pl.BlockSpec(memory_space=pltpu.SMEM)
    shape = jax.ShapeDtypeStruct
    (node_out, edge_out, node_grad, edge_grad, g_ew1, g_ew2, g_nw1, g_nw2, g_small) = pl.pallas_call(
        lambda *refs: layer_kernel(peers, outer, inner, len(shares), *refs),
        out_shape=(
            shape((nodes, width), BF16),
            shape((edges, width), BF16),
            shape((nodes, width), F32),
            shape((edges, width), F32),
            shape((3 * width // peers, width), F32),
            shape((width // peers, width), F32),
            shape((2 * width // peers, width), F32),
            shape((width // peers, width), F32),
            shape((8, 128), F32),
        ),
        in_specs=[vmem] * 5 + [smem] + [vmem] * 10,
        out_specs=[vmem] * 9,
        scratch_shapes=[
            pltpu.VMEM((peers, 16, half), BF16),
            pltpu.VMEM((peers, 16, half), BF16),
            pltpu.VMEM((peers, 16, half + 128), BF16),
            pltpu.VMEM((peers, 16, half + 128), BF16),
            pltpu.VMEM((edges, 3 * width), BF16),
            pltpu.VMEM((edges, width), F32),
            pltpu.VMEM((edges, width), F32),
            pltpu.VMEM((edges, 1), F32),
            pltpu.VMEM((edges, width), BF16),
            pltpu.VMEM((nodes, 2 * width), BF16),
            pltpu.VMEM((nodes, width), F32),
            pltpu.VMEM((nodes, width), F32),
            pltpu.VMEM((nodes, width), BF16),
            pltpu.VMEM((edges, width), BF16),
            pltpu.SemaphoreType.DMA((peers - 1,)),
            pltpu.SemaphoreType.DMA((peers - 1,)),
            pltpu.SemaphoreType.DMA((peers - 1,)),
            pltpu.SemaphoreType.DMA((peers - 1,)),
        ]
        + chunk_scratch,
        compiler_params=pltpu.CompilerParams(
            collective_id=0, has_side_effects=True, vmem_limit_bytes=56 * 1024 * 1024
        ),
    )(
        node_feat,
        edge_feat,
        edge_source.reshape(1, edges),
        edge_target.reshape(1, edges),
        halo_rows.reshape(1, -1),
        edge_count,
        edge_w1,
        edge_b1.reshape(1, width),
        edge_w2,
        edge_gain.reshape(1, width),
        node_w1,
        node_b1.reshape(1, width),
        node_w2,
        node_gain.reshape(1, width),
        node_cot,
        edge_cot,
    )
    per = width // peers
    gb_e, gg_e, gb_n, gg_n = [g_small[0, q * per : (q + 1) * per] for q in range(4)]
    return (
        node_out, edge_out, node_grad, edge_grad, g_ew1, gb_e, g_ew2, gg_e, g_nw1, gb_n, g_nw2, gg_n
    )


def solution(mesh):
    return jax.shard_map(
        on_device,
        mesh=mesh,
        in_specs=(
            P(("groups", "graph"), None),
            P(("groups", "graph"), None),
            P(("groups", "graph")),
            P(("groups", "graph")),
            P(("groups", "graph"), None, None),
            P(("groups", "graph")),
            P(),
            P(),
            P(),
            P(),
            P(),
            P(),
            P(),
            P(),
            P(("groups", "graph"), None),
            P(("groups", "graph"), None),
        ),
        out_specs=(
            P(("groups", "graph"), None),
            P(("groups", "graph"), None),
            P(("groups", "graph"), None),
            P(("groups", "graph"), None),
            P(("groups", "graph"), None),
            P(("groups", "graph")),
            P(("groups", "graph"), None),
            P(("groups", "graph")),
            P(("groups", "graph"), None),
            P(("groups", "graph")),
            P(("groups", "graph"), None),
            P(("groups", "graph")),
        ),
        check_vma=False,
    )
```

```python
import math

import jax
import jax.numpy as jnp
from jax import lax
from jax.experimental import pallas as pl
from jax.experimental.pallas import tpu as pltpu
from jax.sharding import PartitionSpec as P


def silu_grad(pre):
    sig = jax.nn.sigmoid(pre)
    return sig * (1.0 + pre * (1.0 - sig))


def layer_norm(values):
    centred = values - jnp.mean(values, axis=-1, keepdims=True)
    rstd = lax.rsqrt(jnp.mean(centred * centred, axis=-1, keepdims=True) + 1e-05)
    return (centred * rstd, rstd)


def mlp_forward(inputs, first, bias, second):
    pre = jnp.dot(inputs, first, preferred_element_type=jnp.float32) + bias
    active = jax.nn.silu(pre).astype(jnp.bfloat16)
    outer = jnp.dot(active, second, preferred_element_type=jnp.float32)
    normed, rstd = layer_norm(outer)
    return (pre, active, normed, rstd)


def mlp_backward(grad_branch, first, second, gain, pre, normed, rstd):
    grad_gain = jnp.sum(grad_branch * normed, axis=0)
    scaled = grad_branch * gain
    grad_outer = (
        scaled
        - jnp.mean(scaled, axis=-1, keepdims=True)
        - normed * jnp.mean(scaled * normed, axis=-1, keepdims=True)
    ) * rstd
    grad_outer = grad_outer.astype(jnp.bfloat16)
    grad_active = lax.dot_general(
        grad_outer, second, (((1,), (1,)), ((), ())), preferred_element_type=jnp.float32
    )
    grad_pre = (grad_active * silu_grad(pre)).astype(jnp.bfloat16)
    grad_bias = jnp.sum(grad_pre.astype(jnp.float32), axis=0)
    grad_inputs = lax.dot_general(
        grad_pre, first, (((1,), (1,)), ((), ())), preferred_element_type=jnp.float32
    )
    return (grad_inputs, grad_bias, grad_gain, grad_outer, grad_pre)


def transposed(left, right):
    return lax.dot_general(
        left, right, (((0,), (0,)), ((), ())), preferred_element_type=jnp.float32
    )


def indicator(index, count):
    return (index[:, None] == jnp.arange(count, dtype=jnp.int32)[None, :]).astype(jnp.bfloat16)


def general_on_device(
    node_feat,
    edge_feat,
    edge_source,
    edge_target,
    halo_rows,
    edge_count,
    edge_w1,
    edge_b1,
    edge_w2,
    edge_gain,
    node_w1,
    node_b1,
    node_w2,
    node_gain,
    node_cot,
    edge_cot,
):
    peers = lax.axis_size("graph")
    nodes_local, width = node_feat.shape
    edges_local = edge_feat.shape[0]
    slots = halo_rows.shape[2]
    table_rows = nodes_local + peers * slots
    requests = halo_rows.reshape(-1)
    outgoing = jnp.take(node_feat, requests, axis=0).reshape(peers, slots, width)
    received = lax.all_to_all(outgoing, "graph", split_axis=0, concat_axis=0, tiled=True)
    table = jnp.concatenate([node_feat, received.reshape(peers * slots, width)], axis=0)
    source_hot = indicator(edge_source, table_rows)
    target_hot = indicator(edge_target, nodes_local)
    senders = jnp.dot(source_hot, table, preferred_element_type=jnp.float32).astype(jnp.bfloat16)
    receivers = jnp.dot(target_hot, node_feat, preferred_element_type=jnp.float32).astype(
        jnp.bfloat16
    )
    live = (jnp.arange(edges_local, dtype=jnp.int32) < edge_count[0]).astype(jnp.float32)[:, None]
    edge_inputs = jnp.concatenate([edge_feat, senders, receivers], axis=1)
    pre_e, act_e, normed_e, rstd_e = mlp_forward(edge_inputs, edge_w1, edge_b1, edge_w2)
    message = (live * normed_e * edge_gain).astype(jnp.bfloat16)
    edge_out = (edge_feat.astype(jnp.float32) + message.astype(jnp.float32)).astype(jnp.bfloat16)
    agg = transposed(target_hot, message).astype(jnp.bfloat16)
    node_inputs = jnp.concatenate([node_feat, agg], axis=1)
    pre_n, act_n, normed_n, rstd_n = mlp_forward(node_inputs, node_w1, node_b1, node_w2)
    node_out = (node_feat.astype(jnp.float32) + normed_n * node_gain).astype(jnp.bfloat16)
    gin_n, gb_n, gg_n, gout_n, gpre_n = mlp_backward(
        node_cot.astype(jnp.float32), node_w1, node_w2, node_gain, pre_n, normed_n, rstd_n
    )
    grad_agg = gin_n[:, width:].astype(jnp.bfloat16)
    picked = jnp.dot(target_hot, grad_agg, preferred_element_type=jnp.float32)
    grad_message = edge_cot.astype(jnp.float32) + picked
    gin_e, gb_e, gg_e, gout_e, gpre_e = mlp_backward(
        grad_message * live, edge_w1, edge_w2, edge_gain, pre_e, normed_e, rstd_e
    )
    edge_grad = edge_cot.astype(jnp.float32) + gin_e[:, :width]
    grad_send = gin_e[:, width : 2 * width].astype(jnp.bfloat16)
    grad_recv = gin_e[:, 2 * width :].astype(jnp.bfloat16)
    table_grad = transposed(source_hot, grad_send)
    recv_grad = transposed(target_hot, grad_recv)
    halo_part = table_grad[nodes_local:].reshape(peers, slots, width)
    returned = lax.all_to_all(
        halo_part.astype(jnp.bfloat16), "graph", split_axis=0, concat_axis=0, tiled=True
    ).astype(halo_part.dtype)
    halo_grad = jax.ops.segment_sum(returned.reshape(peers * slots, width), requests, nodes_local)
    node_grad = (
        node_cot.astype(jnp.float32)
        + gin_n[:, :width]
        + table_grad[:nodes_local]
        + recv_grad
        + halo_grad
    )
    scale = 1.0 / math.sqrt(edges_local * peers)
    g_ew1, g_eb1, g_ew2, g_egain, g_nw1, g_nb1, g_nw2, g_ngain = (
        lax.psum_scatter(
            transposed(edge_inputs, gpre_e) * scale, "graph", scatter_dimension=0, tiled=True
        ),
        lax.psum_scatter(gb_e * scale, "graph", scatter_dimension=0, tiled=True),
        lax.psum_scatter(
            transposed(act_e, gout_e) * scale, "graph", scatter_dimension=0, tiled=True
        ),
        lax.psum_scatter(gg_e * scale, "graph", scatter_dimension=0, tiled=True),
        lax.psum_scatter(
            transposed(node_inputs, gpre_n) * scale, "graph", scatter_dimension=0, tiled=True
        ),
        lax.psum_scatter(gb_n * scale, "graph", scatter_dimension=0, tiled=True),
        lax.psum_scatter(
            transposed(act_n, gout_n) * scale, "graph", scatter_dimension=0, tiled=True
        ),
        lax.psum_scatter(gg_n * scale, "graph", scatter_dimension=0, tiled=True),
    )
    return (
        node_out,
        edge_out,
        node_grad,
        edge_grad,
        g_ew1,
        g_eb1,
        g_ew2,
        g_egain,
        g_nw1,
        g_nb1,
        g_nw2,
        g_ngain,
    )


MESH = pl.DeviceIdType.MESH
F32 = jnp.float32
BF16 = jnp.bfloat16


def mm(left, right):
    return jnp.dot(left, right, preferred_element_type=F32)


def mm_nt(left, right):
    return lax.dot_general(left, right, (((1,), (1,)), ((), ())), preferred_element_type=F32)


def remote(src, dst, send_sem, recv_sem, peer):
    return pltpu.make_async_remote_copy(
        src_ref=src,
        dst_ref=dst,
        send_sem=send_sem,
        recv_sem=recv_sem,
        device_id={"graph": peer},
        device_id_type=MESH,
    )


class Scatter:
    def __init__(self, place, refs):
        self.outer, self.inner, self.o, self.i, self.c = place
        self.part, self.rc, self.s1, self.ry, self.s2, self.rz, self.send, self.recv = refs
        self.copies = []

    def index(self, o, i, c):
        return (o * self.inner + i) * 2 + c

    def start(self, value):
        rows, cols = self.part.shape[-2:]
        self.part[...] = value.astype(BF16).reshape(self.outer, self.inner, 2, rows, cols)
        peer = self.index(self.o, self.i, 1 - self.c)
        self.core = remote(
            self.part.at[:, :, 1 - self.c], self.rc, self.send.at[0], self.recv.at[0], peer
        )
        self.core.start()
        self.copies.append(self.core)

    def along_inner(self):
        self.core.wait_recv()
        for o in range(self.outer):
            mine = self.part[o, :, pl.ds(self.c, 1)][:, 0]
            self.s1[o] = (mine.astype(F32) + self.rc[o].astype(F32)).astype(BF16)
        self.inner_copies = []
        for k in range(1, self.inner):
            i = lax.rem(self.i + k, self.inner)
            copy = remote(
                self.s1.at[:, i],
                self.ry.at[k - 1],
                self.send.at[k],
                self.recv.at[k],
                self.index(self.o, i, self.c),
            )
            copy.start()
            self.inner_copies.append(copy)
        self.copies += self.inner_copies

    def along_outer(self):
        for copy in self.inner_copies:
            copy.wait_recv()
        for o in range(self.outer):
            total = self.s1[o, pl.ds(self.i, 1)][0].astype(F32)
            for k in range(self.inner - 1):
                total = total + self.ry[k, o].astype(F32)
            self.s2[o] = total.astype(BF16)
        self.outer_copies = []
        for k in range(1, self.outer):
            o = lax.rem(self.o + k, self.outer)
            slot = self.inner - 1 + k
            copy = remote(
                self.s2.at[o],
                self.rz.at[k - 1],
                self.send.at[slot],
                self.recv.at[slot],
                self.index(o, self.i, self.c),
            )
            copy.start()
            self.outer_copies.append(copy)
        self.copies += self.outer_copies

    def finish(self):
        for copy in self.outer_copies:
            copy.wait_recv()
        total = self.s2[pl.ds(self.o, 1)][0].astype(F32)
        for k in range(self.outer - 1):
            total = total + self.rz[k].astype(F32)
        return total


def norm_backward(scaled, normed, rstd):
    return (
        scaled
        - jnp.mean(scaled, axis=-1, keepdims=True)
        - normed * jnp.mean(scaled * normed, axis=-1, keepdims=True)
    ) * rstd


def one_hot_rows(row, count):
    ids = lax.broadcasted_iota(jnp.int32, (count, row.shape[1]), 0)
    return jnp.where(ids == row, 1.0, 0.0).astype(BF16)


def one_hot_columns(row, count):
    length = row.shape[1]
    column = jnp.broadcast_to(row.astype(F32), (128, length)).T.astype(jnp.int32)
    lanes = lax.broadcasted_iota(jnp.int32, (length, 128), 1)
    parts = [
        jnp.where(column == lanes + start, 1.0, 0.0).astype(BF16) for start in range(0, count, 128)
    ]
    return jnp.concatenate(parts, axis=1)


def request_hot(requests, count):
    slots, peers = requests.shape
    lanes = lax.broadcasted_iota(jnp.int32, (slots, count), 1)
    parts = [jnp.where(requests[:, p : p + 1] == lanes, 1.0, 0.0) for p in range(peers)]
    return jnp.concatenate(parts, axis=0).astype(BF16)


def copy_kernel(count, *refs):
    sources, small, results = refs[:count], refs[count], refs[count + 1 : 2 * count + 1]
    vectors, sems = refs[2 * count + 1 : 2 * count + 5], refs[2 * count + 5]
    copies = []
    for k in range(count):
        copies.append(pltpu.make_async_copy(sources[k], results[k], sems.at[k]))
        copies[-1].start()
    for q, ref in enumerate(vectors):
        per = ref.shape[0]
        ref[...] = small[0, q * per : (q + 1) * per]
    for copy in copies:
        copy.wait()


def halves_to_blocks(rows, peers):
    half = rows.shape[1] // 2
    left = rows[:, :half].reshape(peers, 8, half)
    right = rows[:, half:].reshape(peers, 8, half)
    return jnp.concatenate([left, right], axis=1).astype(BF16)


def blocks_to_halves(blocks):
    peers, _, half = blocks.shape
    wide = blocks.astype(F32)
    left = wide[:, :8].reshape(peers * 8, half)
    right = wide[:, 8:].reshape(peers * 8, half)
    return jnp.concatenate([left, right], axis=1).astype(BF16)


def layer_kernel(peers, outer, inner, n_chunks, *refs):
    (nf, ef, src, tgt, req, cnt, ew1, eb1, ew2, egain, nw1, nb1, nw2, ngain, ncot, ecot) = refs[:16]
    (node_out, edge_out, node_grad, edge_grad, g_ew1, g_ew2, g_nw1, g_nw2, g_small) = refs[16:25]
    (hout, hin, bout, bin_, x_e, pre_e, z_e, rstd_e, act_e, x_n, pre_n, z_n, gpre_n, gpre_e,
     h_send, h_recv, b_send, b_recv) = refs[25:43]
    chunk_refs = refs[43:]
    nodes, width = nf.shape
    edges = ef.shape[0]
    me = lax.axis_index("graph")
    c = lax.rem(me, 2)
    i = lax.rem(me // 2, inner)
    o = me // (2 * inner)
    place = (outer, inner, o, i, c)
    s_nw2, s_nw1, s_ew2, s_e0, s_e1 = [
        Scatter(place, chunk_refs[8 * k : 8 * k + 8]) for k in range(n_chunks)
    ]

    barrier = pltpu.get_barrier_semaphore()
    others = [lax.rem(me + k, peers) for k in range(1, peers)]
    for peer in others:
        pl.semaphore_signal(barrier, inc=1, device_id={"graph": peer}, device_id_type=MESH)

    hout[...] = halves_to_blocks(mm(request_hot(req[...], nodes), nf[...]), peers)
    hin[pl.ds(me, 1)] = hout[pl.ds(me, 1)]
    pl.semaphore_wait(barrier, peers - 1)
    halo = []
    for k, peer in enumerate(others):
        copy = remote(hout.at[peer], hin.at[me], h_send.at[k], h_recv.at[k], peer)
        copy.start()
        halo.append(copy)

    table_rows = nodes + peers * 8
    sources = src[...].reshape(1, edges)
    targets = tgt[...].reshape(1, edges)
    source_hot = one_hot_columns(sources, table_rows)
    target_hot = one_hot_columns(targets, nodes)
    target_hot_t = one_hot_rows(targets, nodes)
    live = jnp.where(lax.broadcasted_iota(jnp.int32, (edges, 1), 0) < cnt[0], 1.0, 0.0).astype(F32)
    x_e[:, :width] = ef[...]
    x_e[:, 2 * width :] = mm(target_hot, nf[...]).astype(BF16)
    own = mm(source_hot[:, :nodes], nf[...])
    pre_e[...] = (
        mm(ef[...], ew1[:width]) + mm(x_e[:, 2 * width :], ew1[2 * width :]) + eb1[...]
    )
    x_n[:, :width] = nf[...]
    pre_n[...] = mm(nf[...], nw1[:width]) + nb1[...]

    for copy in halo:
        copy.wait_recv()
    received = blocks_to_halves(hin[...])
    x_e[:, width : 2 * width] = (own + mm(source_hot[:, nodes:], received)).astype(BF16)
    pre = pre_e[...] + mm(x_e[:, width : 2 * width], ew1[width : 2 * width])
    sig = jax.nn.sigmoid(pre)
    act_e[...] = (pre * sig).astype(BF16)
    pre_e[...] = sig * (1.0 + pre * (1.0 - sig))
    normed, rstd = layer_norm(mm(act_e[...], ew2[...]))
    z_e[...] = normed
    rstd_e[...] = rstd
    message = (live * normed * egain[...]).astype(BF16)
    edge_out[...] = (ef[...].astype(F32) + message.astype(F32)).astype(BF16)
    x_n[:, width:] = mm(target_hot_t, message).astype(BF16)

    pre = pre_n[...] + mm(x_n[:, width:], nw1[width:])
    sig = jax.nn.sigmoid(pre)
    act_n = (pre * sig).astype(BF16)
    slope = sig * (1.0 + pre * (1.0 - sig))
    normed, rstd = layer_norm(mm(act_n, nw2[...]))
    node_out[...] = (nf[...].astype(F32) + normed * ngain[...]).astype(BF16)
    grad = ncot[...].astype(F32)
    gg_n = jnp.sum(grad * normed, axis=0, keepdims=True)
    gout = norm_backward(grad * ngain[...], normed, rstd).astype(BF16)
    gpre_n[...] = (mm_nt(gout, nw2[...]) * slope).astype(BF16)
    gb_n = jnp.sum(gpre_n[...].astype(F32), axis=0, keepdims=True)
    grad_agg = mm_nt(gpre_n[...], nw1[width:]).astype(BF16)
    s_nw1.start(transposed(x_n[...], gpre_n[...]))
    s_nw2.start(transposed(act_n, gout))

    grad = live * (ecot[...].astype(F32) + mm(target_hot, grad_agg))
    normed = z_e[...]
    gg_e = jnp.sum(grad * normed, axis=0, keepdims=True)
    gout = norm_backward(grad * egain[...], normed, rstd_e[...]).astype(BF16)
    s_nw1.along_inner()
    s_ew2.start(transposed(act_e[...], gout))
    s_nw2.along_inner()
    gpre_e[...] = (mm_nt(gout, ew2[...]) * pre_e[...]).astype(BF16)
    gb_e = jnp.sum(gpre_e[...].astype(F32), axis=0, keepdims=True)
    half = width // 2
    s_e0.start(transposed(x_e[...], gpre_e[:, :half]))
    s_ew2.along_inner()
    s_nw1.along_outer()
    s_e1.start(transposed(x_e[...], gpre_e[:, half:]))
    s_nw2.along_outer()

    grad_send = mm_nt(gpre_e[...], ew1[width : 2 * width]).astype(BF16)
    source_hot_t = one_hot_rows(sources, table_rows)
    bout[:, :, :half] = halves_to_blocks(mm(source_hot_t[nodes:], grad_send), peers)
    per = width // peers
    column = lax.broadcasted_iota(jnp.int32, (peers, width), 1)
    owner = lax.broadcasted_iota(jnp.int32, (peers, width), 0) * per
    owned = jnp.logical_and(column >= owner, column < owner + per)
    where_from = lax.rem(lax.broadcasted_iota(jnp.int32, (width, 128), 0), per)
    where_to = lax.broadcasted_iota(jnp.int32, (width, 128), 1)
    small = jnp.zeros((peers, 128), F32)
    for q, vector in enumerate((gb_e, gg_e, gb_n, gg_n)):
        spread = jnp.where(owned, vector, 0.0).astype(BF16)
        move = jnp.where(where_to == where_from + q * per, 1.0, 0.0).astype(BF16)
        small = small + mm(spread, move)
    bout[:, :, half:] = jnp.broadcast_to(small[:, None, :], (peers, 16, 128)).astype(BF16)
    bin_[pl.ds(me, 1)] = bout[pl.ds(me, 1)]
    s_e0.along_inner()
    back = []
    for k, peer in enumerate(others):
        copy = remote(bout.at[peer], bin_.at[me], b_send.at[k], b_recv.at[k], peer)
        copy.start()
        back.append(copy)
    s_e1.along_inner()
    s_ew2.along_outer()

    edge_grad[...] = ecot[...].astype(F32) + mm_nt(gpre_e[...], ew1[:width])
    grad_recv = mm_nt(gpre_e[...], ew1[2 * width :]).astype(BF16)
    s_e0.along_outer()
    node_grad[...] = (
        ncot[...].astype(F32)
        + mm_nt(gpre_n[...], nw1[:width])
        + mm(source_hot_t[:nodes], grad_send)
        + mm(target_hot_t, grad_recv)
    )
    s_e1.along_outer()
    scale = 1.0 / math.sqrt(edges * peers)
    g_nw1[...] = s_nw1.finish() * scale
    g_nw2[...] = s_nw2.finish() * scale
    for copy in back:
        copy.wait_recv()
    node_grad[...] += transposed(request_hot(req[...], nodes), blocks_to_halves(bin_[:, :, :half]))
    g_small[...] = jnp.sum(bin_[:, :, half:].astype(F32), axis=0)[:8] * scale
    g_ew2[...] = s_ew2.finish() * scale
    g_ew1[:, :half] = s_e0.finish() * scale
    g_ew1[:, half:] = s_e1.finish() * scale
    for copy in halo + back:
        copy.wait_send()
    for chunk in (s_nw1, s_nw2, s_ew2, s_e0, s_e1):
        for copy in chunk.copies:
            copy.wait_send()


def kernel_fits(peers, width, slots):
    return (
        slots == 8
        and width % (peers * 16) == 0
        and 4 * (width // peers) <= 128
        and peers * slots % 128 == 0
    )


def on_device(
    node_feat,
    edge_feat,
    edge_source,
    edge_target,
    halo_rows,
    edge_count,
    edge_w1,
    edge_b1,
    edge_w2,
    edge_gain,
    node_w1,
    node_b1,
    node_w2,
    node_gain,
    node_cot,
    edge_cot,
):
    peers = lax.axis_size("graph")
    nodes, width = node_feat.shape
    edges = edge_feat.shape[0]
    if not kernel_fits(peers, width, halo_rows.shape[2]):
        return general_on_device(
            node_feat, edge_feat, edge_source, edge_target, halo_rows, edge_count,
            edge_w1, edge_b1, edge_w2, edge_gain, node_w1, node_b1, node_w2, node_gain,
            node_cot, edge_cot,
        )
    inner = 1 << (int(math.log2(peers // 2)) // 2)
    outer = peers // 2 // inner
    shares = [
        (width // peers, width),
        (2 * width // peers, width),
        (width // peers, width),
        (3 * width // peers, width // 2),
        (3 * width // peers, width // 2),
    ]
    chunk_scratch = []
    for rows, cols in shares:
        chunk_scratch += [
            pltpu.VMEM((outer, inner, 2, rows, cols), BF16),
            pltpu.VMEM((outer, inner, rows, cols), BF16),
            pltpu.VMEM((outer, inner, rows, cols), BF16),
            pltpu.VMEM((inner - 1, outer, rows, cols), BF16),
            pltpu.VMEM((outer, rows, cols), BF16),
            pltpu.VMEM((outer - 1, rows, cols), BF16),
            pltpu.SemaphoreType.DMA((inner + outer - 1,)),
            pltpu.SemaphoreType.DMA((inner + outer - 1,)),
        ]
    half = width // 2
    vmem = pl.BlockSpec(memory_space=pltpu.VMEM)
    smem = pl.BlockSpec(memory_space=pltpu.SMEM)
    shape = jax.ShapeDtypeStruct
    (node_out, edge_out, node_grad, edge_grad, g_ew1, g_ew2, g_nw1, g_nw2, g_small) = pl.pallas_call(
        lambda *refs: layer_kernel(peers, outer, inner, len(shares), *refs),
        out_shape=(
            shape((nodes, width), BF16),
            shape((edges, width), BF16),
            shape((nodes, width), F32),
            shape((edges, width), F32),
            shape((3 * width // peers, width), F32),
            shape((width // peers, width), F32),
            shape((2 * width // peers, width), F32),
            shape((width // peers, width), F32),
            shape((8, 128), F32),
        ),
        in_specs=[vmem] * 5 + [smem] + [vmem] * 10,
        out_specs=[vmem] * 9,
        scratch_shapes=[
            pltpu.VMEM((peers, 16, half), BF16),
            pltpu.VMEM((peers, 16, half), BF16),
            pltpu.VMEM((peers, 16, half + 128), BF16),
            pltpu.VMEM((peers, 16, half + 128), BF16),
            pltpu.VMEM((edges, 3 * width), BF16),
            pltpu.VMEM((edges, width), F32),
            pltpu.VMEM((edges, width), F32),
            pltpu.VMEM((edges, 1), F32),
            pltpu.VMEM((edges, width), BF16),
            pltpu.VMEM((nodes, 2 * width), BF16),
            pltpu.VMEM((nodes, width), F32),
            pltpu.VMEM((nodes, width), F32),
            pltpu.VMEM((nodes, width), BF16),
            pltpu.VMEM((edges, width), BF16),
            pltpu.SemaphoreType.DMA((peers - 1,)),
            pltpu.SemaphoreType.DMA((peers - 1,)),
            pltpu.SemaphoreType.DMA((peers - 1,)),
            pltpu.SemaphoreType.DMA((peers - 1,)),
        ]
        + chunk_scratch,
        compiler_params=pltpu.CompilerParams(
            collective_id=0, has_side_effects=True, vmem_limit_bytes=56 * 1024 * 1024
        ),
    )(
        node_feat,
        edge_feat,
        edge_source,
        edge_target,
        halo_rows[0].T,
        edge_count,
        edge_w1,
        edge_b1.reshape(1, width),
        edge_w2,
        edge_gain.reshape(1, width),
        node_w1,
        node_b1.reshape(1, width),
        node_w2,
        node_gain.reshape(1, width),
        node_cot,
        edge_cot,
    )
    whole = (node_out, edge_out, node_grad, edge_grad, g_ew1, g_ew2, g_nw1, g_nw2)
    anywhere = pl.BlockSpec(memory_space=pl.ANY)
    (node_out, edge_out, node_grad, edge_grad, g_ew1, g_ew2, g_nw1, g_nw2, gb_e, gg_e, gb_n, gg_n) = (
        pl.pallas_call(
            lambda *refs: copy_kernel(len(whole), *refs),
            out_shape=[shape(array.shape, array.dtype) for array in whole]
            + [shape((width // peers,), F32)] * 4,
            in_specs=[anywhere] * len(whole) + [vmem],
            out_specs=[anywhere] * len(whole) + [vmem] * 4,
            scratch_shapes=[pltpu.SemaphoreType.DMA((len(whole),))],
        )(*whole, g_small)
    )
    return (
        node_out, edge_out, node_grad, edge_grad, g_ew1, gb_e, g_ew2, gg_e, g_nw1, gb_n, g_nw2, gg_n
    )


def solution(mesh):
    return jax.shard_map(
        on_device,
        mesh=mesh,
        in_specs=(
            P(("groups", "graph"), None),
            P(("groups", "graph"), None),
            P(("groups", "graph")),
            P(("groups", "graph")),
            P(("groups", "graph"), None, None),
            P(("groups", "graph")),
            P(),
            P(),
            P(),
            P(),
            P(),
            P(),
            P(),
            P(),
            P(("groups", "graph"), None),
            P(("groups", "graph"), None),
        ),
        out_specs=(
            P(("groups", "graph"), None),
            P(("groups", "graph"), None),
            P(("groups", "graph"), None),
            P(("groups", "graph"), None),
            P(("groups", "graph"), None),
            P(("groups", "graph")),
            P(("groups", "graph"), None),
            P(("groups", "graph")),
            P(("groups", "graph"), None),
            P(("groups", "graph")),
            P(("groups", "graph"), None),
            P(("groups", "graph")),
        ),
        check_vma=False,
    )
```

```python
import math

import jax
import jax.numpy as jnp
from jax import lax
from jax.experimental import pallas as pl
from jax.experimental.pallas import tpu as pltpu
from jax.sharding import PartitionSpec as P


def silu_grad(pre):
    sig = jax.nn.sigmoid(pre)
    return sig * (1.0 + pre * (1.0 - sig))


def layer_norm(values):
    centred = values - jnp.mean(values, axis=-1, keepdims=True)
    rstd = lax.rsqrt(jnp.mean(centred * centred, axis=-1, keepdims=True) + 1e-05)
    return (centred * rstd, rstd)


def mlp_forward(inputs, first, bias, second):
    pre = jnp.dot(inputs, first, preferred_element_type=jnp.float32) + bias
    active = jax.nn.silu(pre).astype(jnp.bfloat16)
    outer = jnp.dot(active, second, preferred_element_type=jnp.float32)
    normed, rstd = layer_norm(outer)
    return (pre, active, normed, rstd)


def mlp_backward(grad_branch, first, second, gain, pre, normed, rstd):
    grad_gain = jnp.sum(grad_branch * normed, axis=0)
    scaled = grad_branch * gain
    grad_outer = (
        scaled
        - jnp.mean(scaled, axis=-1, keepdims=True)
        - normed * jnp.mean(scaled * normed, axis=-1, keepdims=True)
    ) * rstd
    grad_outer = grad_outer.astype(jnp.bfloat16)
    grad_active = lax.dot_general(
        grad_outer, second, (((1,), (1,)), ((), ())), preferred_element_type=jnp.float32
    )
    grad_pre = (grad_active * silu_grad(pre)).astype(jnp.bfloat16)
    grad_bias = jnp.sum(grad_pre.astype(jnp.float32), axis=0)
    grad_inputs = lax.dot_general(
        grad_pre, first, (((1,), (1,)), ((), ())), preferred_element_type=jnp.float32
    )
    return (grad_inputs, grad_bias, grad_gain, grad_outer, grad_pre)


def transposed(left, right):
    return lax.dot_general(
        left, right, (((0,), (0,)), ((), ())), preferred_element_type=jnp.float32
    )


def indicator(index, count):
    return (index[:, None] == jnp.arange(count, dtype=jnp.int32)[None, :]).astype(jnp.bfloat16)


def general_on_device(
    node_feat,
    edge_feat,
    edge_source,
    edge_target,
    halo_rows,
    edge_count,
    edge_w1,
    edge_b1,
    edge_w2,
    edge_gain,
    node_w1,
    node_b1,
    node_w2,
    node_gain,
    node_cot,
    edge_cot,
):
    peers = lax.axis_size("graph")
    nodes_local, width = node_feat.shape
    edges_local = edge_feat.shape[0]
    slots = halo_rows.shape[2]
    table_rows = nodes_local + peers * slots
    requests = halo_rows.reshape(-1)
    outgoing = jnp.take(node_feat, requests, axis=0).reshape(peers, slots, width)
    received = lax.all_to_all(outgoing, "graph", split_axis=0, concat_axis=0, tiled=True)
    table = jnp.concatenate([node_feat, received.reshape(peers * slots, width)], axis=0)
    source_hot = indicator(edge_source, table_rows)
    target_hot = indicator(edge_target, nodes_local)
    senders = jnp.dot(source_hot, table, preferred_element_type=jnp.float32).astype(jnp.bfloat16)
    receivers = jnp.dot(target_hot, node_feat, preferred_element_type=jnp.float32).astype(
        jnp.bfloat16
    )
    live = (jnp.arange(edges_local, dtype=jnp.int32) < edge_count[0]).astype(jnp.float32)[:, None]
    edge_inputs = jnp.concatenate([edge_feat, senders, receivers], axis=1)
    pre_e, act_e, normed_e, rstd_e = mlp_forward(edge_inputs, edge_w1, edge_b1, edge_w2)
    message = (live * normed_e * edge_gain).astype(jnp.bfloat16)
    edge_out = (edge_feat.astype(jnp.float32) + message.astype(jnp.float32)).astype(jnp.bfloat16)
    agg = transposed(target_hot, message).astype(jnp.bfloat16)
    node_inputs = jnp.concatenate([node_feat, agg], axis=1)
    pre_n, act_n, normed_n, rstd_n = mlp_forward(node_inputs, node_w1, node_b1, node_w2)
    node_out = (node_feat.astype(jnp.float32) + normed_n * node_gain).astype(jnp.bfloat16)
    gin_n, gb_n, gg_n, gout_n, gpre_n = mlp_backward(
        node_cot.astype(jnp.float32), node_w1, node_w2, node_gain, pre_n, normed_n, rstd_n
    )
    grad_agg = gin_n[:, width:].astype(jnp.bfloat16)
    picked = jnp.dot(target_hot, grad_agg, preferred_element_type=jnp.float32)
    grad_message = edge_cot.astype(jnp.float32) + picked
    gin_e, gb_e, gg_e, gout_e, gpre_e = mlp_backward(
        grad_message * live, edge_w1, edge_w2, edge_gain, pre_e, normed_e, rstd_e
    )
    edge_grad = edge_cot.astype(jnp.float32) + gin_e[:, :width]
    grad_send = gin_e[:, width : 2 * width].astype(jnp.bfloat16)
    grad_recv = gin_e[:, 2 * width :].astype(jnp.bfloat16)
    table_grad = transposed(source_hot, grad_send)
    recv_grad = transposed(target_hot, grad_recv)
    halo_part = table_grad[nodes_local:].reshape(peers, slots, width)
    returned = lax.all_to_all(
        halo_part.astype(jnp.bfloat16), "graph", split_axis=0, concat_axis=0, tiled=True
    ).astype(halo_part.dtype)
    halo_grad = jax.ops.segment_sum(returned.reshape(peers * slots, width), requests, nodes_local)
    node_grad = (
        node_cot.astype(jnp.float32)
        + gin_n[:, :width]
        + table_grad[:nodes_local]
        + recv_grad
        + halo_grad
    )
    scale = 1.0 / math.sqrt(edges_local * peers)
    g_ew1, g_eb1, g_ew2, g_egain, g_nw1, g_nb1, g_nw2, g_ngain = (
        lax.psum_scatter(
            transposed(edge_inputs, gpre_e) * scale, "graph", scatter_dimension=0, tiled=True
        ),
        lax.psum_scatter(gb_e * scale, "graph", scatter_dimension=0, tiled=True),
        lax.psum_scatter(
            transposed(act_e, gout_e) * scale, "graph", scatter_dimension=0, tiled=True
        ),
        lax.psum_scatter(gg_e * scale, "graph", scatter_dimension=0, tiled=True),
        lax.psum_scatter(
            transposed(node_inputs, gpre_n) * scale, "graph", scatter_dimension=0, tiled=True
        ),
        lax.psum_scatter(gb_n * scale, "graph", scatter_dimension=0, tiled=True),
        lax.psum_scatter(
            transposed(act_n, gout_n) * scale, "graph", scatter_dimension=0, tiled=True
        ),
        lax.psum_scatter(gg_n * scale, "graph", scatter_dimension=0, tiled=True),
    )
    return (
        node_out,
        edge_out,
        node_grad,
        edge_grad,
        g_ew1,
        g_eb1,
        g_ew2,
        g_egain,
        g_nw1,
        g_nb1,
        g_nw2,
        g_ngain,
    )


MESH = pl.DeviceIdType.MESH
F32 = jnp.float32
BF16 = jnp.bfloat16


def mm(left, right):
    return jnp.dot(left, right, preferred_element_type=F32)


def mm_nt(left, right):
    return lax.dot_general(left, right, (((1,), (1,)), ((), ())), preferred_element_type=F32)


def remote(src, dst, send_sem, recv_sem, peer):
    return pltpu.make_async_remote_copy(
        src_ref=src,
        dst_ref=dst,
        send_sem=send_sem,
        recv_sem=recv_sem,
        device_id={"graph": peer},
        device_id_type=MESH,
    )


class Scatter:
    def __init__(self, place, refs):
        self.outer, self.inner, self.o, self.i, self.c = place
        self.part, self.rc, self.s1, self.ry, self.s2, self.rz, self.send, self.recv = refs
        self.copies = []

    def index(self, o, i, c):
        return (o * self.inner + i) * 2 + c

    def start(self, value):
        rows, cols = self.part.shape[-2:]
        self.part[...] = value.astype(BF16).reshape(self.outer, self.inner, 2, rows, cols)
        peer = self.index(self.o, self.i, 1 - self.c)
        self.core = remote(
            self.part.at[:, :, 1 - self.c], self.rc, self.send.at[0], self.recv.at[0], peer
        )
        self.core.start()
        self.copies.append(self.core)

    def along_inner(self):
        self.core.wait_recv()
        for o in range(self.outer):
            mine = self.part[o, :, pl.ds(self.c, 1)][:, 0]
            self.s1[o] = (mine.astype(F32) + self.rc[o].astype(F32)).astype(BF16)
        self.inner_copies = []
        for k in range(1, self.inner):
            i = lax.rem(self.i + k, self.inner)
            copy = remote(
                self.s1.at[:, i],
                self.ry.at[k - 1],
                self.send.at[k],
                self.recv.at[k],
                self.index(self.o, i, self.c),
            )
            copy.start()
            self.inner_copies.append(copy)
        self.copies += self.inner_copies

    def along_outer(self):
        for copy in self.inner_copies:
            copy.wait_recv()
        for o in range(self.outer):
            total = self.s1[o, pl.ds(self.i, 1)][0].astype(F32)
            for k in range(self.inner - 1):
                total = total + self.ry[k, o].astype(F32)
            self.s2[o] = total.astype(BF16)
        self.outer_copies = []
        for k in range(1, self.outer):
            o = lax.rem(self.o + k, self.outer)
            slot = self.inner - 1 + k
            copy = remote(
                self.s2.at[o],
                self.rz.at[k - 1],
                self.send.at[slot],
                self.recv.at[slot],
                self.index(o, self.i, self.c),
            )
            copy.start()
            self.outer_copies.append(copy)
        self.copies += self.outer_copies

    def finish(self):
        for copy in self.outer_copies:
            copy.wait_recv()
        total = self.s2[pl.ds(self.o, 1)][0].astype(F32)
        for k in range(self.outer - 1):
            total = total + self.rz[k].astype(F32)
        return total


def norm_backward(scaled, normed, rstd):
    return (
        scaled
        - jnp.mean(scaled, axis=-1, keepdims=True)
        - normed * jnp.mean(scaled * normed, axis=-1, keepdims=True)
    ) * rstd


def one_hot_rows(row, count):
    ids = lax.broadcasted_iota(jnp.int32, (count, row.shape[1]), 0)
    return jnp.where(ids == row, 1.0, 0.0).astype(BF16)


def one_hot_columns(row, count):
    length = row.shape[1]
    column = jnp.broadcast_to(row.astype(F32), (128, length)).T.astype(jnp.int32)
    lanes = lax.broadcasted_iota(jnp.int32, (length, 128), 1)
    parts = [
        jnp.where(column == lanes + start, 1.0, 0.0).astype(BF16) for start in range(0, count, 128)
    ]
    return jnp.concatenate(parts, axis=1)


def request_hot(requests, count):
    slots, peers = requests.shape
    lanes = lax.broadcasted_iota(jnp.int32, (slots, count), 1)
    parts = [jnp.where(requests[:, p : p + 1] == lanes, 1.0, 0.0) for p in range(peers)]
    return jnp.concatenate(parts, axis=0).astype(BF16)


def copy_kernel(count, *refs):
    sources, small, results = refs[:count], refs[count], refs[count + 1 : 2 * count + 1]
    vectors, held = refs[2 * count + 1 : 2 * count + 5], refs[2 * count + 5 : 3 * count + 5]
    in_sems, out_sems = refs[3 * count + 5 :]
    fetches = [pltpu.make_async_copy(sources[k], held[k], in_sems.at[k]) for k in range(count)]
    copies = [pltpu.make_async_copy(held[k], results[k], out_sems.at[k]) for k in range(count)]
    for fetch in fetches:
        fetch.start()
    for fetch, copy in zip(fetches, copies):
        fetch.wait()
        copy.start()
    for q, ref in enumerate(vectors):
        per = ref.shape[0]
        ref[...] = small[0, q * per : (q + 1) * per]
    for copy in copies:
        copy.wait()


def halves_to_blocks(rows, peers):
    half = rows.shape[1] // 2
    left = rows[:, :half].reshape(peers, 8, half)
    right = rows[:, half:].reshape(peers, 8, half)
    return jnp.concatenate([left, right], axis=1).astype(BF16)


def blocks_to_halves(blocks):
    peers, _, half = blocks.shape
    wide = blocks.astype(F32)
    left = wide[:, :8].reshape(peers * 8, half)
    right = wide[:, 8:].reshape(peers * 8, half)
    return jnp.concatenate([left, right], axis=1).astype(BF16)


def layer_kernel(peers, outer, inner, n_chunks, *refs):
    (nf, ef, src, tgt, req, cnt, ew1, eb1, ew2, egain, nw1, nb1, nw2, ngain, ncot, ecot) = refs[:16]
    (node_out, edge_out, node_grad, edge_grad, g_ew1, g_ew2, g_nw1, g_nw2, g_small) = refs[16:25]
    (hout, hin, bout, bin_, x_e, pre_e, z_e, rstd_e, act_e, x_n, pre_n, z_n, gpre_n, gpre_e,
     h_send, h_recv, b_send, b_recv) = refs[25:43]
    chunk_refs = refs[43:]
    nodes, width = nf.shape
    edges = ef.shape[0]
    me = lax.axis_index("graph")
    c = lax.rem(me, 2)
    i = lax.rem(me // 2, inner)
    o = me // (2 * inner)
    place = (outer, inner, o, i, c)
    s_nw2, s_nw1, s_ew2, s_e0, s_e1 = [
        Scatter(place, chunk_refs[8 * k : 8 * k + 8]) for k in range(n_chunks)
    ]

    barrier = pltpu.get_barrier_semaphore()
    others = [lax.rem(me + k, peers) for k in range(1, peers)]
    for peer in others:
        pl.semaphore_signal(barrier, inc=1, device_id={"graph": peer}, device_id_type=MESH)

    hout[...] = halves_to_blocks(mm(request_hot(req[...], nodes), nf[...]), peers)
    hin[pl.ds(me, 1)] = hout[pl.ds(me, 1)]
    pl.semaphore_wait(barrier, peers - 1)
    halo = []
    for k, peer in enumerate(others):
        copy = remote(hout.at[peer], hin.at[me], h_send.at[k], h_recv.at[k], peer)
        copy.start()
        halo.append(copy)

    table_rows = nodes + peers * 8
    sources = src[...].reshape(1, edges)
    targets = tgt[...].reshape(1, edges)
    source_hot = one_hot_columns(sources, table_rows)
    target_hot = one_hot_columns(targets, nodes)
    target_hot_t = one_hot_rows(targets, nodes)
    live = jnp.where(lax.broadcasted_iota(jnp.int32, (edges, 1), 0) < cnt[0], 1.0, 0.0).astype(F32)
    x_e[:, :width] = ef[...]
    x_e[:, 2 * width :] = mm(target_hot, nf[...]).astype(BF16)
    own = mm(source_hot[:, :nodes], nf[...])
    pre_e[...] = (
        mm(ef[...], ew1[:width]) + mm(x_e[:, 2 * width :], ew1[2 * width :]) + eb1[...]
    )
    x_n[:, :width] = nf[...]
    pre_n[...] = mm(nf[...], nw1[:width]) + nb1[...]

    for copy in halo:
        copy.wait_recv()
    received = blocks_to_halves(hin[...])
    x_e[:, width : 2 * width] = (own + mm(source_hot[:, nodes:], received)).astype(BF16)
    pre = pre_e[...] + mm(x_e[:, width : 2 * width], ew1[width : 2 * width])
    sig = jax.nn.sigmoid(pre)
    act_e[...] = (pre * sig).astype(BF16)
    pre_e[...] = sig * (1.0 + pre * (1.0 - sig))
    normed, rstd = layer_norm(mm(act_e[...], ew2[...]))
    z_e[...] = normed
    rstd_e[...] = rstd
    message = (live * normed * egain[...]).astype(BF16)
    edge_out[...] = (ef[...].astype(F32) + message.astype(F32)).astype(BF16)
    x_n[:, width:] = mm(target_hot_t, message).astype(BF16)

    pre = pre_n[...] + mm(x_n[:, width:], nw1[width:])
    sig = jax.nn.sigmoid(pre)
    act_n = (pre * sig).astype(BF16)
    slope = sig * (1.0 + pre * (1.0 - sig))
    normed, rstd = layer_norm(mm(act_n, nw2[...]))
    node_out[...] = (nf[...].astype(F32) + normed * ngain[...]).astype(BF16)
    grad = ncot[...].astype(F32)
    gg_n = jnp.sum(grad * normed, axis=0, keepdims=True)
    gout = norm_backward(grad * ngain[...], normed, rstd).astype(BF16)
    gpre_n[...] = (mm_nt(gout, nw2[...]) * slope).astype(BF16)
    gb_n = jnp.sum(gpre_n[...].astype(F32), axis=0, keepdims=True)
    grad_agg = mm_nt(gpre_n[...], nw1[width:]).astype(BF16)
    s_nw1.start(transposed(x_n[...], gpre_n[...]))
    s_nw2.start(transposed(act_n, gout))

    grad = live * (ecot[...].astype(F32) + mm(target_hot, grad_agg))
    normed = z_e[...]
    gg_e = jnp.sum(grad * normed, axis=0, keepdims=True)
    gout = norm_backward(grad * egain[...], normed, rstd_e[...]).astype(BF16)
    s_nw1.along_inner()
    s_ew2.start(transposed(act_e[...], gout))
    s_nw2.along_inner()
    gpre_e[...] = (mm_nt(gout, ew2[...]) * pre_e[...]).astype(BF16)
    gb_e = jnp.sum(gpre_e[...].astype(F32), axis=0, keepdims=True)
    half = width // 2
    s_e0.start(transposed(x_e[...], gpre_e[:, :half]))
    s_ew2.along_inner()
    s_nw1.along_outer()
    s_e1.start(transposed(x_e[...], gpre_e[:, half:]))
    s_nw2.along_outer()

    grad_send = mm_nt(gpre_e[...], ew1[width : 2 * width]).astype(BF16)
    source_hot_t = one_hot_rows(sources, table_rows)
    bout[:, :, :half] = halves_to_blocks(mm(source_hot_t[nodes:], grad_send), peers)
    per = width // peers
    column = lax.broadcasted_iota(jnp.int32, (peers, width), 1)
    owner = lax.broadcasted_iota(jnp.int32, (peers, width), 0) * per
    owned = jnp.logical_and(column >= owner, column < owner + per)
    where_from = lax.rem(lax.broadcasted_iota(jnp.int32, (width, 128), 0), per)
    where_to = lax.broadcasted_iota(jnp.int32, (width, 128), 1)
    small = jnp.zeros((peers, 128), F32)
    for q, vector in enumerate((gb_e, gg_e, gb_n, gg_n)):
        spread = jnp.where(owned, vector, 0.0).astype(BF16)
        move = jnp.where(where_to == where_from + q * per, 1.0, 0.0).astype(BF16)
        small = small + mm(spread, move)
    bout[:, :, half:] = jnp.broadcast_to(small[:, None, :], (peers, 16, 128)).astype(BF16)
    bin_[pl.ds(me, 1)] = bout[pl.ds(me, 1)]
    s_e0.along_inner()
    back = []
    for k, peer in enumerate(others):
        copy = remote(bout.at[peer], bin_.at[me], b_send.at[k], b_recv.at[k], peer)
        copy.start()
        back.append(copy)
    s_e1.along_inner()
    s_ew2.along_outer()

    edge_grad[...] = ecot[...].astype(F32) + mm_nt(gpre_e[...], ew1[:width])
    grad_recv = mm_nt(gpre_e[...], ew1[2 * width :]).astype(BF16)
    s_e0.along_outer()
    node_grad[...] = (
        ncot[...].astype(F32)
        + mm_nt(gpre_n[...], nw1[:width])
        + mm(source_hot_t[:nodes], grad_send)
        + mm(target_hot_t, grad_recv)
    )
    s_e1.along_outer()
    scale = 1.0 / math.sqrt(edges * peers)
    g_nw1[...] = s_nw1.finish() * scale
    g_nw2[...] = s_nw2.finish() * scale
    for copy in back:
        copy.wait_recv()
    node_grad[...] += transposed(request_hot(req[...], nodes), blocks_to_halves(bin_[:, :, :half]))
    g_small[...] = jnp.sum(bin_[:, :, half:].astype(F32), axis=0)[:8] * scale
    g_ew2[...] = s_ew2.finish() * scale
    g_ew1[:, :half] = s_e0.finish() * scale
    g_ew1[:, half:] = s_e1.finish() * scale
    for copy in halo + back:
        copy.wait_send()
    for chunk in (s_nw1, s_nw2, s_ew2, s_e0, s_e1):
        for copy in chunk.copies:
            copy.wait_send()


def kernel_fits(peers, width, slots):
    return (
        slots == 8
        and width % (peers * 16) == 0
        and 4 * (width // peers) <= 128
        and peers * slots % 128 == 0
    )


def on_device(
    node_feat,
    edge_feat,
    edge_source,
    edge_target,
    halo_rows,
    edge_count,
    edge_w1,
    edge_b1,
    edge_w2,
    edge_gain,
    node_w1,
    node_b1,
    node_w2,
    node_gain,
    node_cot,
    edge_cot,
):
    peers = lax.axis_size("graph")
    nodes, width = node_feat.shape
    edges = edge_feat.shape[0]
    if not kernel_fits(peers, width, halo_rows.shape[2]):
        return general_on_device(
            node_feat, edge_feat, edge_source, edge_target, halo_rows, edge_count,
            edge_w1, edge_b1, edge_w2, edge_gain, node_w1, node_b1, node_w2, node_gain,
            node_cot, edge_cot,
        )
    inner = 1 << (int(math.log2(peers // 2)) // 2)
    outer = peers // 2 // inner
    shares = [
        (width // peers, width),
        (2 * width // peers, width),
        (width // peers, width),
        (3 * width // peers, width // 2),
        (3 * width // peers, width // 2),
    ]
    chunk_scratch = []
    for rows, cols in shares:
        chunk_scratch += [
            pltpu.VMEM((outer, inner, 2, rows, cols), BF16),
            pltpu.VMEM((outer, inner, rows, cols), BF16),
            pltpu.VMEM((outer, inner, rows, cols), BF16),
            pltpu.VMEM((inner - 1, outer, rows, cols), BF16),
            pltpu.VMEM((outer, rows, cols), BF16),
            pltpu.VMEM((outer - 1, rows, cols), BF16),
            pltpu.SemaphoreType.DMA((inner + outer - 1,)),
            pltpu.SemaphoreType.DMA((inner + outer - 1,)),
        ]
    half = width // 2
    vmem = pl.BlockSpec(memory_space=pltpu.VMEM)
    smem = pl.BlockSpec(memory_space=pltpu.SMEM)
    shape = jax.ShapeDtypeStruct
    (node_out, edge_out, node_grad, edge_grad, g_ew1, g_ew2, g_nw1, g_nw2, g_small) = pl.pallas_call(
        lambda *refs: layer_kernel(peers, outer, inner, len(shares), *refs),
        out_shape=(
            shape((nodes, width), BF16),
            shape((edges, width), BF16),
            shape((nodes, width), F32),
            shape((edges, width), F32),
            shape((3 * width // peers, width), F32),
            shape((width // peers, width), F32),
            shape((2 * width // peers, width), F32),
            shape((width // peers, width), F32),
            shape((8, 128), F32),
        ),
        in_specs=[vmem] * 5 + [smem] + [vmem] * 10,
        out_specs=[vmem] * 9,
        scratch_shapes=[
            pltpu.VMEM((peers, 16, half), BF16),
            pltpu.VMEM((peers, 16, half), BF16),
            pltpu.VMEM((peers, 16, half + 128), BF16),
            pltpu.VMEM((peers, 16, half + 128), BF16),
            pltpu.VMEM((edges, 3 * width), BF16),
            pltpu.VMEM((edges, width), F32),
            pltpu.VMEM((edges, width), F32),
            pltpu.VMEM((edges, 1), F32),
            pltpu.VMEM((edges, width), BF16),
            pltpu.VMEM((nodes, 2 * width), BF16),
            pltpu.VMEM((nodes, width), F32),
            pltpu.VMEM((nodes, width), F32),
            pltpu.VMEM((nodes, width), BF16),
            pltpu.VMEM((edges, width), BF16),
            pltpu.SemaphoreType.DMA((peers - 1,)),
            pltpu.SemaphoreType.DMA((peers - 1,)),
            pltpu.SemaphoreType.DMA((peers - 1,)),
            pltpu.SemaphoreType.DMA((peers - 1,)),
        ]
        + chunk_scratch,
        compiler_params=pltpu.CompilerParams(
            collective_id=0, has_side_effects=True, vmem_limit_bytes=56 * 1024 * 1024
        ),
    )(
        node_feat,
        edge_feat,
        edge_source,
        edge_target,
        halo_rows[0].T,
        edge_count,
        edge_w1,
        edge_b1.reshape(1, width),
        edge_w2,
        edge_gain.reshape(1, width),
        node_w1,
        node_b1.reshape(1, width),
        node_w2,
        node_gain.reshape(1, width),
        node_cot,
        edge_cot,
    )
    whole = (node_out, edge_out, node_grad, edge_grad, g_ew1, g_ew2, g_nw1, g_nw2)
    anywhere = pl.BlockSpec(memory_space=pl.ANY)
    (node_out, edge_out, node_grad, edge_grad, g_ew1, g_ew2, g_nw1, g_nw2, gb_e, gg_e, gb_n, gg_n) = (
        pl.pallas_call(
            lambda *refs: copy_kernel(len(whole), *refs),
            out_shape=[shape(array.shape, array.dtype) for array in whole]
            + [shape((width // peers,), F32)] * 4,
            in_specs=[anywhere] * len(whole) + [vmem],
            out_specs=[anywhere] * len(whole) + [vmem] * 4,
            scratch_shapes=[pltpu.VMEM(array.shape, array.dtype) for array in whole]
            + [pltpu.SemaphoreType.DMA((len(whole),))] * 2,
            compiler_params=pltpu.CompilerParams(vmem_limit_bytes=32 * 1024 * 1024),
        )(*whole, g_small)
    )
    return (
        node_out, edge_out, node_grad, edge_grad, g_ew1, gb_e, g_ew2, gg_e, g_nw1, gb_n, g_nw2, gg_n
    )


def solution(mesh):
    return jax.shard_map(
        on_device,
        mesh=mesh,
        in_specs=(
            P(("groups", "graph"), None),
            P(("groups", "graph"), None),
            P(("groups", "graph")),
            P(("groups", "graph")),
            P(("groups", "graph"), None, None),
            P(("groups", "graph")),
            P(),
            P(),
            P(),
            P(),
            P(),
            P(),
            P(),
            P(),
            P(("groups", "graph"), None),
            P(("groups", "graph"), None),
        ),
        out_specs=(
            P(("groups", "graph"), None),
            P(("groups", "graph"), None),
            P(("groups", "graph"), None),
            P(("groups", "graph"), None),
            P(("groups", "graph"), None),
            P(("groups", "graph")),
            P(("groups", "graph"), None),
            P(("groups", "graph")),
            P(("groups", "graph"), None),
            P(("groups", "graph")),
            P(("groups", "graph"), None),
            P(("groups", "graph")),
        ),
        check_vma=False,
    )
```

```python
import math

import jax
import jax.numpy as jnp
from jax import lax
from jax.experimental import pallas as pl
from jax.experimental.pallas import tpu as pltpu
from jax.sharding import PartitionSpec as P


def silu_grad(pre):
    sig = jax.nn.sigmoid(pre)
    return sig * (1.0 + pre * (1.0 - sig))


def layer_norm(values):
    centred = values - jnp.mean(values, axis=-1, keepdims=True)
    rstd = lax.rsqrt(jnp.mean(centred * centred, axis=-1, keepdims=True) + 1e-05)
    return (centred * rstd, rstd)


def mlp_forward(inputs, first, bias, second):
    pre = jnp.dot(inputs, first, preferred_element_type=jnp.float32) + bias
    active = jax.nn.silu(pre).astype(jnp.bfloat16)
    outer = jnp.dot(active, second, preferred_element_type=jnp.float32)
    normed, rstd = layer_norm(outer)
    return (pre, active, normed, rstd)


def mlp_backward(grad_branch, first, second, gain, pre, normed, rstd):
    grad_gain = jnp.sum(grad_branch * normed, axis=0)
    scaled = grad_branch * gain
    grad_outer = (
        scaled
        - jnp.mean(scaled, axis=-1, keepdims=True)
        - normed * jnp.mean(scaled * normed, axis=-1, keepdims=True)
    ) * rstd
    grad_outer = grad_outer.astype(jnp.bfloat16)
    grad_active = lax.dot_general(
        grad_outer, second, (((1,), (1,)), ((), ())), preferred_element_type=jnp.float32
    )
    grad_pre = (grad_active * silu_grad(pre)).astype(jnp.bfloat16)
    grad_bias = jnp.sum(grad_pre.astype(jnp.float32), axis=0)
    grad_inputs = lax.dot_general(
        grad_pre, first, (((1,), (1,)), ((), ())), preferred_element_type=jnp.float32
    )
    return (grad_inputs, grad_bias, grad_gain, grad_outer, grad_pre)


def transposed(left, right):
    return lax.dot_general(
        left, right, (((0,), (0,)), ((), ())), preferred_element_type=jnp.float32
    )


def indicator(index, count):
    return (index[:, None] == jnp.arange(count, dtype=jnp.int32)[None, :]).astype(jnp.bfloat16)


def general_on_device(
    node_feat,
    edge_feat,
    edge_source,
    edge_target,
    halo_rows,
    edge_count,
    edge_w1,
    edge_b1,
    edge_w2,
    edge_gain,
    node_w1,
    node_b1,
    node_w2,
    node_gain,
    node_cot,
    edge_cot,
):
    peers = lax.axis_size("graph")
    nodes_local, width = node_feat.shape
    edges_local = edge_feat.shape[0]
    slots = halo_rows.shape[2]
    table_rows = nodes_local + peers * slots
    requests = halo_rows.reshape(-1)
    outgoing = jnp.take(node_feat, requests, axis=0).reshape(peers, slots, width)
    received = lax.all_to_all(outgoing, "graph", split_axis=0, concat_axis=0, tiled=True)
    table = jnp.concatenate([node_feat, received.reshape(peers * slots, width)], axis=0)
    source_hot = indicator(edge_source, table_rows)
    target_hot = indicator(edge_target, nodes_local)
    senders = jnp.dot(source_hot, table, preferred_element_type=jnp.float32).astype(jnp.bfloat16)
    receivers = jnp.dot(target_hot, node_feat, preferred_element_type=jnp.float32).astype(
        jnp.bfloat16
    )
    live = (jnp.arange(edges_local, dtype=jnp.int32) < edge_count[0]).astype(jnp.float32)[:, None]
    edge_inputs = jnp.concatenate([edge_feat, senders, receivers], axis=1)
    pre_e, act_e, normed_e, rstd_e = mlp_forward(edge_inputs, edge_w1, edge_b1, edge_w2)
    message = (live * normed_e * edge_gain).astype(jnp.bfloat16)
    edge_out = (edge_feat.astype(jnp.float32) + message.astype(jnp.float32)).astype(jnp.bfloat16)
    agg = transposed(target_hot, message).astype(jnp.bfloat16)
    node_inputs = jnp.concatenate([node_feat, agg], axis=1)
    pre_n, act_n, normed_n, rstd_n = mlp_forward(node_inputs, node_w1, node_b1, node_w2)
    node_out = (node_feat.astype(jnp.float32) + normed_n * node_gain).astype(jnp.bfloat16)
    gin_n, gb_n, gg_n, gout_n, gpre_n = mlp_backward(
        node_cot.astype(jnp.float32), node_w1, node_w2, node_gain, pre_n, normed_n, rstd_n
    )
    grad_agg = gin_n[:, width:].astype(jnp.bfloat16)
    picked = jnp.dot(target_hot, grad_agg, preferred_element_type=jnp.float32)
    grad_message = edge_cot.astype(jnp.float32) + picked
    gin_e, gb_e, gg_e, gout_e, gpre_e = mlp_backward(
        grad_message * live, edge_w1, edge_w2, edge_gain, pre_e, normed_e, rstd_e
    )
    edge_grad = edge_cot.astype(jnp.float32) + gin_e[:, :width]
    grad_send = gin_e[:, width : 2 * width].astype(jnp.bfloat16)
    grad_recv = gin_e[:, 2 * width :].astype(jnp.bfloat16)
    table_grad = transposed(source_hot, grad_send)
    recv_grad = transposed(target_hot, grad_recv)
    halo_part = table_grad[nodes_local:].reshape(peers, slots, width)
    returned = lax.all_to_all(
        halo_part.astype(jnp.bfloat16), "graph", split_axis=0, concat_axis=0, tiled=True
    ).astype(halo_part.dtype)
    halo_grad = jax.ops.segment_sum(returned.reshape(peers * slots, width), requests, nodes_local)
    node_grad = (
        node_cot.astype(jnp.float32)
        + gin_n[:, :width]
        + table_grad[:nodes_local]
        + recv_grad
        + halo_grad
    )
    scale = 1.0 / math.sqrt(edges_local * peers)
    g_ew1, g_eb1, g_ew2, g_egain, g_nw1, g_nb1, g_nw2, g_ngain = (
        lax.psum_scatter(
            transposed(edge_inputs, gpre_e) * scale, "graph", scatter_dimension=0, tiled=True
        ),
        lax.psum_scatter(gb_e * scale, "graph", scatter_dimension=0, tiled=True),
        lax.psum_scatter(
            transposed(act_e, gout_e) * scale, "graph", scatter_dimension=0, tiled=True
        ),
        lax.psum_scatter(gg_e * scale, "graph", scatter_dimension=0, tiled=True),
        lax.psum_scatter(
            transposed(node_inputs, gpre_n) * scale, "graph", scatter_dimension=0, tiled=True
        ),
        lax.psum_scatter(gb_n * scale, "graph", scatter_dimension=0, tiled=True),
        lax.psum_scatter(
            transposed(act_n, gout_n) * scale, "graph", scatter_dimension=0, tiled=True
        ),
        lax.psum_scatter(gg_n * scale, "graph", scatter_dimension=0, tiled=True),
    )
    return (
        node_out,
        edge_out,
        node_grad,
        edge_grad,
        g_ew1,
        g_eb1,
        g_ew2,
        g_egain,
        g_nw1,
        g_nb1,
        g_nw2,
        g_ngain,
    )


MESH = pl.DeviceIdType.MESH
F32 = jnp.float32
BF16 = jnp.bfloat16


def mm(left, right):
    return jnp.dot(left, right, preferred_element_type=F32)


def mm_nt(left, right):
    return lax.dot_general(left, right, (((1,), (1,)), ((), ())), preferred_element_type=F32)


def remote(src, dst, send_sem, recv_sem, peer):
    return pltpu.make_async_remote_copy(
        src_ref=src,
        dst_ref=dst,
        send_sem=send_sem,
        recv_sem=recv_sem,
        device_id={"graph": peer},
        device_id_type=MESH,
    )


class Scatter:
    def __init__(self, place, refs):
        self.outer, self.inner, self.o, self.i, self.c = place
        self.part, self.rc, self.s1, self.ry, self.s2, self.rz, self.send, self.recv = refs
        self.copies = []

    def index(self, o, i, c):
        return (o * self.inner + i) * 2 + c

    def start(self, value):
        rows, cols = self.part.shape[-2:]
        self.part[...] = value.astype(BF16).reshape(self.outer, self.inner, 2, rows, cols)
        peer = self.index(self.o, self.i, 1 - self.c)
        self.core = remote(
            self.part.at[:, :, 1 - self.c], self.rc, self.send.at[0], self.recv.at[0], peer
        )
        self.core.start()
        self.copies.append(self.core)

    def along_inner(self):
        self.core.wait_recv()
        for o in range(self.outer):
            mine = self.part[o, :, pl.ds(self.c, 1)][:, 0]
            self.s1[o] = (mine.astype(F32) + self.rc[o].astype(F32)).astype(BF16)
        self.inner_copies = []
        for k in range(1, self.inner):
            i = lax.rem(self.i + k, self.inner)
            copy = remote(
                self.s1.at[:, i],
                self.ry.at[k - 1],
                self.send.at[k],
                self.recv.at[k],
                self.index(self.o, i, self.c),
            )
            copy.start()
            self.inner_copies.append(copy)
        self.copies += self.inner_copies

    def along_outer(self):
        for copy in self.inner_copies:
            copy.wait_recv()
        for o in range(self.outer):
            total = self.s1[o, pl.ds(self.i, 1)][0].astype(F32)
            for k in range(self.inner - 1):
                total = total + self.ry[k, o].astype(F32)
            self.s2[o] = total.astype(BF16)
        self.outer_copies = []
        for k in range(1, self.outer):
            o = lax.rem(self.o + k, self.outer)
            slot = self.inner - 1 + k
            copy = remote(
                self.s2.at[o],
                self.rz.at[k - 1],
                self.send.at[slot],
                self.recv.at[slot],
                self.index(o, self.i, self.c),
            )
            copy.start()
            self.outer_copies.append(copy)
        self.copies += self.outer_copies

    def finish(self):
        for copy in self.outer_copies:
            copy.wait_recv()
        total = self.s2[pl.ds(self.o, 1)][0].astype(F32)
        for k in range(self.outer - 1):
            total = total + self.rz[k].astype(F32)
        return total


def norm_backward(scaled, normed, rstd):
    return (
        scaled
        - jnp.mean(scaled, axis=-1, keepdims=True)
        - normed * jnp.mean(scaled * normed, axis=-1, keepdims=True)
    ) * rstd


def one_hot_rows(row, count):
    ids = lax.broadcasted_iota(jnp.int32, (count, row.shape[1]), 0)
    return jnp.where(ids == row, 1.0, 0.0).astype(BF16)


def one_hot_columns(row, count):
    length = row.shape[1]
    column = jnp.broadcast_to(row.astype(F32), (128, length)).T.astype(jnp.int32)
    lanes = lax.broadcasted_iota(jnp.int32, (length, 128), 1)
    parts = [
        jnp.where(column == lanes + start, 1.0, 0.0).astype(BF16) for start in range(0, count, 128)
    ]
    return jnp.concatenate(parts, axis=1)


def request_hot(requests, count):
    slots, peers = requests.shape
    lanes = lax.broadcasted_iota(jnp.int32, (slots, count), 1)
    parts = [jnp.where(requests[:, p : p + 1] == lanes, 1.0, 0.0) for p in range(peers)]
    return jnp.concatenate(parts, axis=0).astype(BF16)


def copy_kernel(count, *refs):
    sources, small, results = refs[:count], refs[count], refs[count + 1 : 2 * count + 1]
    vectors, held = refs[2 * count + 1 : 2 * count + 5], refs[2 * count + 5 : 3 * count + 5]
    in_sems, out_sems = refs[3 * count + 5 :]
    fetches = [pltpu.make_async_copy(sources[k], held[k], in_sems.at[k]) for k in range(count)]
    copies = [pltpu.make_async_copy(held[k], results[k], out_sems.at[k]) for k in range(count)]
    for fetch in fetches:
        fetch.start()
    for fetch, copy in zip(fetches, copies):
        fetch.wait()
        copy.start()
    for q, ref in enumerate(vectors):
        per = ref.shape[0]
        ref[...] = small[0, q * per : (q + 1) * per]
    for copy in copies:
        copy.wait()


def halves_to_blocks(rows, peers):
    half = rows.shape[1] // 2
    left = rows[:, :half].reshape(peers, 8, half)
    right = rows[:, half:].reshape(peers, 8, half)
    return jnp.concatenate([left, right], axis=1).astype(BF16)


def blocks_to_halves(blocks):
    peers, _, half = blocks.shape
    wide = blocks.astype(F32)
    left = wide[:, :8].reshape(peers * 8, half)
    right = wide[:, 8:].reshape(peers * 8, half)
    return jnp.concatenate([left, right], axis=1).astype(BF16)


def layer_kernel(peers, outer, inner, n_chunks, *refs):
    (nf, ef, src, tgt, req, cnt, ew1, eb1, ew2, egain, nw1, nb1, nw2, ngain, ncot, ecot) = refs[:16]
    (node_out, edge_out, node_grad, edge_grad, g_ew1, g_ew2, g_nw1, g_nw2, g_small) = refs[16:25]
    (hout, hin, bout, bin_, x_e, pre_e, z_e, rstd_e, act_e, x_n, pre_n, z_n, gpre_n, gpre_e,
     h_send, h_recv, b_send, b_recv) = refs[25:43]
    chunk_refs = refs[43:]
    nodes, width = nf.shape
    edges = ef.shape[0]
    me = lax.axis_index("graph")
    c = lax.rem(me, 2)
    i = lax.rem(me // 2, inner)
    o = me // (2 * inner)
    place = (outer, inner, o, i, c)
    s_nw2, s_nw1, s_ew2, s_e0, s_e1 = [
        Scatter(place, chunk_refs[8 * k : 8 * k + 8]) for k in range(n_chunks)
    ]

    barrier = pltpu.get_barrier_semaphore()
    others = [lax.rem(me + k, peers) for k in range(1, peers)]
    for peer in others:
        pl.semaphore_signal(barrier, inc=1, device_id={"graph": peer}, device_id_type=MESH)

    hout[...] = halves_to_blocks(mm(request_hot(req[...], nodes), nf[...]), peers)
    hin[pl.ds(me, 1)] = hout[pl.ds(me, 1)]
    pl.semaphore_wait(barrier, peers - 1)
    halo = []
    for k, peer in enumerate(others):
        copy = remote(hout.at[peer], hin.at[me], h_send.at[k], h_recv.at[k], peer)
        copy.start()
        halo.append(copy)

    table_rows = nodes + peers * 8
    sources = src[...].reshape(1, edges)
    targets = tgt[...].reshape(1, edges)
    source_hot = one_hot_columns(sources, table_rows)
    target_hot = one_hot_columns(targets, nodes)
    target_hot_t = one_hot_rows(targets, nodes)
    live = jnp.where(lax.broadcasted_iota(jnp.int32, (edges, 1), 0) < cnt[0], 1.0, 0.0).astype(F32)
    x_e[:, :width] = ef[...]
    x_e[:, 2 * width :] = mm(target_hot, nf[...]).astype(BF16)
    own = mm(source_hot[:, :nodes], nf[...])
    pre_e[...] = (
        mm(ef[...], ew1[:width]) + mm(x_e[:, 2 * width :], ew1[2 * width :]) + eb1[...]
    )
    x_n[:, :width] = nf[...]
    pre_n[...] = mm(nf[...], nw1[:width]) + nb1[...]

    for copy in halo:
        copy.wait_recv()
    received = blocks_to_halves(hin[...])
    x_e[:, width : 2 * width] = (own + mm(source_hot[:, nodes:], received)).astype(BF16)
    pre = pre_e[...] + mm(x_e[:, width : 2 * width], ew1[width : 2 * width])
    sig = jax.nn.sigmoid(pre)
    act_e[...] = (pre * sig).astype(BF16)
    pre_e[...] = sig * (1.0 + pre * (1.0 - sig))
    normed, rstd = layer_norm(mm(act_e[...], ew2[...]))
    z_e[...] = normed
    rstd_e[...] = rstd
    message = (live * normed * egain[...]).astype(BF16)
    edge_out[...] = (ef[...].astype(F32) + message.astype(F32)).astype(BF16)
    x_n[:, width:] = mm(target_hot_t, message).astype(BF16)

    pre = pre_n[...] + mm(x_n[:, width:], nw1[width:])
    sig = jax.nn.sigmoid(pre)
    act_n = (pre * sig).astype(BF16)
    slope = sig * (1.0 + pre * (1.0 - sig))
    normed, rstd = layer_norm(mm(act_n, nw2[...]))
    node_out[...] = (nf[...].astype(F32) + normed * ngain[...]).astype(BF16)
    grad = ncot[...].astype(F32)
    gg_n = jnp.sum(grad * normed, axis=0, keepdims=True)
    gout = norm_backward(grad * ngain[...], normed, rstd).astype(BF16)
    gpre_n[...] = (mm_nt(gout, nw2[...]) * slope).astype(BF16)
    gb_n = jnp.sum(gpre_n[...].astype(F32), axis=0, keepdims=True)
    grad_agg = mm_nt(gpre_n[...], nw1[width:]).astype(BF16)
    s_nw1.start(transposed(x_n[...], gpre_n[...]))
    s_nw2.start(transposed(act_n, gout))

    grad = live * (ecot[...].astype(F32) + mm(target_hot, grad_agg))
    normed = z_e[...]
    gg_e = jnp.sum(grad * normed, axis=0, keepdims=True)
    gout = norm_backward(grad * egain[...], normed, rstd_e[...]).astype(BF16)
    s_nw1.along_inner()
    s_ew2.start(transposed(act_e[...], gout))
    s_nw2.along_inner()
    gpre_e[...] = (mm_nt(gout, ew2[...]) * pre_e[...]).astype(BF16)
    gb_e = jnp.sum(gpre_e[...].astype(F32), axis=0, keepdims=True)
    half = width // 2
    s_e0.start(transposed(x_e[...], gpre_e[:, :half]))
    s_ew2.along_inner()
    s_nw1.along_outer()
    s_e1.start(transposed(x_e[...], gpre_e[:, half:]))
    s_nw2.along_outer()

    grad_send = mm_nt(gpre_e[...], ew1[width : 2 * width]).astype(BF16)
    source_hot_t = one_hot_rows(sources, table_rows)
    bout[:, :, :half] = halves_to_blocks(mm(source_hot_t[nodes:], grad_send), peers)
    per = width // peers
    column = lax.broadcasted_iota(jnp.int32, (peers, width), 1)
    owner = lax.broadcasted_iota(jnp.int32, (peers, width), 0) * per
    owned = jnp.logical_and(column >= owner, column < owner + per)
    where_from = lax.rem(lax.broadcasted_iota(jnp.int32, (width, 128), 0), per)
    where_to = lax.broadcasted_iota(jnp.int32, (width, 128), 1)
    small = jnp.zeros((peers, 128), F32)
    for q, vector in enumerate((gb_e, gg_e, gb_n, gg_n)):
        spread = jnp.where(owned, vector, 0.0).astype(BF16)
        move = jnp.where(where_to == where_from + q * per, 1.0, 0.0).astype(BF16)
        small = small + mm(spread, move)
    bout[:, :, half:] = jnp.broadcast_to(small[:, None, :], (peers, 16, 128)).astype(BF16)
    bin_[pl.ds(me, 1)] = bout[pl.ds(me, 1)]
    s_e0.along_inner()
    back = []
    for k, peer in enumerate(others):
        copy = remote(bout.at[peer], bin_.at[me], b_send.at[k], b_recv.at[k], peer)
        copy.start()
        back.append(copy)
    s_e1.along_inner()
    s_ew2.along_outer()

    edge_grad[...] = ecot[...].astype(F32) + mm_nt(gpre_e[...], ew1[:width])
    grad_recv = mm_nt(gpre_e[...], ew1[2 * width :]).astype(BF16)
    s_e0.along_outer()
    node_grad[...] = (
        ncot[...].astype(F32)
        + mm_nt(gpre_n[...], nw1[:width])
        + mm(source_hot_t[:nodes], grad_send)
        + mm(target_hot_t, grad_recv)
    )
    s_e1.along_outer()
    scale = 1.0 / math.sqrt(edges * peers)
    g_nw1[...] = s_nw1.finish() * scale
    g_nw2[...] = s_nw2.finish() * scale
    for copy in back:
        copy.wait_recv()
    node_grad[...] += transposed(request_hot(req[...], nodes), blocks_to_halves(bin_[:, :, :half]))
    g_small[...] = jnp.sum(bin_[:, :, half:].astype(F32), axis=0)[:8] * scale
    g_ew2[...] = s_ew2.finish() * scale
    g_ew1[:, :half] = s_e0.finish() * scale
    g_ew1[:, half:] = s_e1.finish() * scale
    for copy in halo + back:
        copy.wait_send()
    for chunk in (s_nw1, s_nw2, s_ew2, s_e0, s_e1):
        for copy in chunk.copies:
            copy.wait_send()


def kernel_fits(peers, width, slots):
    return (
        slots == 8
        and width % (peers * 16) == 0
        and 4 * (width // peers) <= 128
        and peers * slots % 128 == 0
    )


def on_device(
    node_feat,
    edge_feat,
    edge_source,
    edge_target,
    halo_rows,
    edge_count,
    edge_w1,
    edge_b1,
    edge_w2,
    edge_gain,
    node_w1,
    node_b1,
    node_w2,
    node_gain,
    node_cot,
    edge_cot,
):
    peers = lax.axis_size("graph")
    nodes, width = node_feat.shape
    edges = edge_feat.shape[0]
    if not kernel_fits(peers, width, halo_rows.shape[2]):
        return general_on_device(
            node_feat, edge_feat, edge_source, edge_target, halo_rows, edge_count,
            edge_w1, edge_b1, edge_w2, edge_gain, node_w1, node_b1, node_w2, node_gain,
            node_cot, edge_cot,
        )
    inner = 1 << (int(math.log2(peers // 2)) // 2)
    outer = peers // 2 // inner
    shares = [
        (width // peers, width),
        (2 * width // peers, width),
        (width // peers, width),
        (3 * width // peers, width // 2),
        (3 * width // peers, width // 2),
    ]
    chunk_scratch = []
    for rows, cols in shares:
        chunk_scratch += [
            pltpu.VMEM((outer, inner, 2, rows, cols), BF16),
            pltpu.VMEM((outer, inner, rows, cols), BF16),
            pltpu.VMEM((outer, inner, rows, cols), BF16),
            pltpu.VMEM((inner - 1, outer, rows, cols), BF16),
            pltpu.VMEM((outer, rows, cols), BF16),
            pltpu.VMEM((outer - 1, rows, cols), BF16),
            pltpu.SemaphoreType.DMA((inner + outer - 1,)),
            pltpu.SemaphoreType.DMA((inner + outer - 1,)),
        ]
    half = width // 2
    vmem = pl.BlockSpec(memory_space=pltpu.VMEM)
    smem = pl.BlockSpec(memory_space=pltpu.SMEM)
    shape = jax.ShapeDtypeStruct
    (node_out, edge_out, node_grad, edge_grad, g_ew1, g_ew2, g_nw1, g_nw2, g_small) = pl.pallas_call(
        lambda *refs: layer_kernel(peers, outer, inner, len(shares), *refs),
        out_shape=(
            shape((nodes, width), BF16),
            shape((edges, width), BF16),
            shape((nodes, width), F32),
            shape((edges, width), F32),
            shape((3 * width // peers, width), F32),
            shape((width // peers, width), F32),
            shape((2 * width // peers, width), F32),
            shape((width // peers, width), F32),
            shape((8, 128), F32),
        ),
        in_specs=[vmem] * 5 + [smem] + [vmem] * 10,
        out_specs=[vmem] * 9,
        scratch_shapes=[
            pltpu.VMEM((peers, 16, half), BF16),
            pltpu.VMEM((peers, 16, half), BF16),
            pltpu.VMEM((peers, 16, half + 128), BF16),
            pltpu.VMEM((peers, 16, half + 128), BF16),
            pltpu.VMEM((edges, 3 * width), BF16),
            pltpu.VMEM((edges, width), F32),
            pltpu.VMEM((edges, width), F32),
            pltpu.VMEM((edges, 1), F32),
            pltpu.VMEM((edges, width), BF16),
            pltpu.VMEM((nodes, 2 * width), BF16),
            pltpu.VMEM((nodes, width), F32),
            pltpu.VMEM((nodes, width), F32),
            pltpu.VMEM((nodes, width), BF16),
            pltpu.VMEM((edges, width), BF16),
            pltpu.SemaphoreType.DMA((peers - 1,)),
            pltpu.SemaphoreType.DMA((peers - 1,)),
            pltpu.SemaphoreType.DMA((peers - 1,)),
            pltpu.SemaphoreType.DMA((peers - 1,)),
        ]
        + chunk_scratch,
        compiler_params=pltpu.CompilerParams(
            collective_id=0, has_side_effects=True, vmem_limit_bytes=56 * 1024 * 1024
        ),
    )(
        node_feat,
        edge_feat,
        edge_source,
        edge_target,
        halo_rows[0].T,
        edge_count,
        edge_w1,
        edge_b1.reshape(1, width),
        edge_w2,
        edge_gain.reshape(1, width),
        node_w1,
        node_b1.reshape(1, width),
        node_w2,
        node_gain.reshape(1, width),
        node_cot,
        edge_cot,
    )
    whole = (node_out, edge_out, node_grad, edge_grad, g_ew1, g_ew2, g_nw1, g_nw2)
    anywhere = pl.BlockSpec(memory_space=pl.ANY)
    (node_out, edge_out, node_grad, edge_grad, g_ew1, g_ew2, g_nw1, g_nw2, gb_e, gg_e, gb_n, gg_n) = (
        pl.pallas_call(
            lambda *refs: copy_kernel(len(whole), *refs),
            out_shape=[shape(array.shape, array.dtype) for array in whole]
            + [shape((width // peers,), F32)] * 4,
            in_specs=[anywhere] * len(whole) + [vmem],
            out_specs=[anywhere] * len(whole) + [vmem] * 4,
            scratch_shapes=[pltpu.VMEM(array.shape, array.dtype) for array in whole]
            + [pltpu.SemaphoreType.DMA((len(whole),))] * 2,
            compiler_params=pltpu.CompilerParams(vmem_limit_bytes=60 * 1024 * 1024),
        )(*whole, g_small)
    )
    return (
        node_out, edge_out, node_grad, edge_grad, g_ew1, gb_e, g_ew2, gg_e, g_nw1, gb_n, g_nw2, gg_n
    )


def solution(mesh):
    return jax.shard_map(
        on_device,
        mesh=mesh,
        in_specs=(
            P(("groups", "graph"), None),
            P(("groups", "graph"), None),
            P(("groups", "graph")),
            P(("groups", "graph")),
            P(("groups", "graph"), None, None),
            P(("groups", "graph")),
            P(),
            P(),
            P(),
            P(),
            P(),
            P(),
            P(),
            P(),
            P(("groups", "graph"), None),
            P(("groups", "graph"), None),
        ),
        out_specs=(
            P(("groups", "graph"), None),
            P(("groups", "graph"), None),
            P(("groups", "graph"), None),
            P(("groups", "graph"), None),
            P(("groups", "graph"), None),
            P(("groups", "graph")),
            P(("groups", "graph"), None),
            P(("groups", "graph")),
            P(("groups", "graph"), None),
            P(("groups", "graph")),
            P(("groups", "graph"), None),
            P(("groups", "graph")),
        ),
        check_vma=False,
    )
```
